512 devices in a mesh: ctx: 8 (over x, core), exp: 64 (over y, z).
Axes of the slice: x: 4, y: 8, z: 8, core: 2. Of those that a mesh axis runs over, the one named last changes fastest.
Arguments:
- queries: float32 [64, 2048, 128], P('exp', 'ctx'), may hold values from -0.5 to 0.5
- key_vectors: float32 [64, 2048, 128], P('exp', 'ctx'), may hold values from -1 to 1, as said below
- values: float32 [64, 2048, 128], P('exp', 'ctx'), may hold values from -6 to 6
- out_gate: float32 [64, 2048, 128], P('exp', 'ctx'), may hold values from -6 to 6
- write_strength: float32 [64, 2048], P('exp', 'ctx'), may hold values from 0.2 to 0.9
- log_fading_factor: float32 [64, 2048], P('exp', 'ctx'), may hold values from -2 to 0
- block_inverse: float32 [64, 32, 64, 64], P('exp', 'ctx'), may hold values from -1 to 1, as said below
- norm_gain: float32 [128], replicated, may hold values from 0.5 to 1.5
- hidden: bfloat16 [65536, 1024], P(('ctx', 'exp')), may hold values from -6 to 6
- routes: int32 [65536, 10], P(('ctx', 'exp')), may hold values from 0 to 511, all different within a row; in each aligned block of 128 rows (0 to 127, 128 to 255, ...) at most 3 rows name the same one
- route_weights: float32 [65536, 10], P(('ctx', 'exp')), may hold values from 0.1 to 1.9
- gate_weights: bfloat16 [512, 1024, 512], P(('ctx', 'exp')), may hold values from -0.1875 to 0.1875
- up_weights: bfloat16 [512, 1024, 512], P(('ctx', 'exp')), may hold values from -0.1875 to 0.1875
- down_weights: bfloat16 [512, 512, 1024], P(('ctx', 'exp')), may hold values from -0.25 to 0.25
Outputs:
- mixer_output: float32 [64, 2048, 128], P('exp', 'ctx')
- expert_output: bfloat16 [65536, 1024], P(('ctx', 'exp'))
The draws below stay inside these ranges and needn't reach their ends.
Inputs may be any that keep to these rules, and one draw needn't show every extreme that they name: `routes`: each row names 10 different experts. Among the 128 rows of one device no expert is named more than 3 times, and in every draw some expert is named exactly 3 times by one device's rows. `key_vectors`: every row has Euclidean length 1. `block_inverse`: each block's matrix has ones on its diagonal and zeros above it.
All inputs are finite; a program needn't handle non-finite values.
Results may differ from the reference program's by a relative error of at most 0.0058.
Values may be sent and summed in bfloat16 or wider, within the bound.
No kernel may reach another device: no remote copies, remote signals or barrier semaphores. Data moves between devices by JAX's collectives and lax.ppermute only.
A program may use at most 128 MiB of HBM per device.

```python
import math
import jax
import jax.numpy as jnp
import numpy as np
from jax import lax

D = 1024
MOE_FF = 512
HEAD_DIM = 128
BLOCK = 64
TOP = 10
PART_SPAN = 256
TOK_DEV = 128
LANE_TOTAL = 64
STRING_SPAN = 2048
EXPERTS = 512
TOKENS = 65536
CAP = 3
DEVICES = 512


def track_parts(key, slow_share):
    split_sampler_seeds = jax.random.split(key, 9)
    normal_rows = jax.random.normal(split_sampler_seeds[0], (LANE_TOTAL, STRING_SPAN, HEAD_DIM), jnp.float32)
    key_vectors = normal_rows / jnp.sqrt(jnp.sum(normal_rows * normal_rows, axis=-1, keepdims=True))
    strength = jax.random.uniform(split_sampler_seeds[1], (LANE_TOTAL, STRING_SPAN), jnp.float32, 0.2, 0.9)
    slow_track = jax.random.bernoulli(split_sampler_seeds[2], slow_share, (LANE_TOTAL,))
    fast_rate = jnp.exp(jax.random.uniform(split_sampler_seeds[3], (LANE_TOTAL,), jnp.float32, math.log(1.0 / 50.0), math.log(1.0 / 30.0)))
    slow_rate = jnp.exp(jax.random.uniform(split_sampler_seeds[4], (LANE_TOTAL,), jnp.float32, math.log(0.2 / STRING_SPAN), math.log(0.8 / STRING_SPAN)))
    resting_intensity = jnp.where(slow_track, slow_rate, fast_rate)
    piecewise_scaling_factor = jnp.exp(jax.random.uniform(split_sampler_seeds[5], (LANE_TOTAL, STRING_SPAN // PART_SPAN), jnp.float32, math.log(0.5), math.log(2.0)))
    entry_scaling_factor = jnp.exp(jax.random.uniform(split_sampler_seeds[6], (LANE_TOTAL, STRING_SPAN), jnp.float32, math.log(0.5), math.log(2.0)))
    spike_onset = jax.random.randint(split_sampler_seeds[7], (LANE_TOTAL, 2), 0, STRING_SPAN)
    spike_duration = jax.random.uniform(split_sampler_seeds[8], (LANE_TOTAL, 2), jnp.float32, 0.22, 0.69)
    place_ordinal = jnp.arange(STRING_SPAN)
    spike_occurrences = jnp.sum(jnp.where(place_ordinal[None, None, :] == spike_onset[:, :, None], spike_duration[:, :, None], 0.0), axis=1)
    log_fading_factor = -(resting_intensity[:, None] * jnp.repeat(piecewise_scaling_factor, PART_SPAN, axis=1) * entry_scaling_factor) - spike_occurrences
    return (key_vectors, strength, log_fading_factor)


def draw_key_vectors(key, part):
    slow_share = 0.5
    return track_parts(key, slow_share)[0]


def draw_write_strength(key, part):
    slow_share = 0.5
    return track_parts(key, slow_share)[1]


def draw_log_fading_factor(key, part):
    slow_share = 0.5
    return track_parts(key, slow_share)[2]


def draw_block_inverse(key, part):
    key = jax.random.fold_in(key, 7)
    blocks = STRING_SPAN // BLOCK
    entries = jax.random.uniform(key, (LANE_TOTAL, blocks, BLOCK, BLOCK), jnp.float32, -0.12, 0.12)
    row_index = lax.broadcasted_iota(jnp.int32, (BLOCK, BLOCK), 0)
    col_index = lax.broadcasted_iota(jnp.int32, (BLOCK, BLOCK), 1)
    lower_part = jnp.where(row_index > col_index, entries, 0.0)
    diagonal = jnp.where(row_index == col_index, 1.0, 0.0)
    return (lower_part + diagonal).astype(jnp.float32)


def levels(own_key, extent, cuts, least, high):
    def one(axis_at, blocks):
        heights = jax.random.uniform(jax.random.fold_in(jax.random.fold_in(own_key, 6), axis_at), (blocks,), jnp.float32, least / len(cuts), high / len(cuts))
        return jnp.repeat(jnp.exp(heights), extent[axis_at] // blocks).reshape((-1,) + (1,) * (len(extent) - axis_at - 1))

    gain = one(*cuts[0])
    for cut in cuts[1:]:
        gain = gain * one(*cut)
    return gain


def assign_block(stream_key, own, number, rows, amount, top, limit, slope):
    order = jax.random.permutation(stream_key, amount)
    crowded, usual = shares(amount, rows * top, limit, slope, True), shares(amount, rows * top, limit, slope, False)
    places = jnp.arange(amount)

    def named(lengths, offset_by):
        used = int((lengths > 0).sum())
        fixed = max(1, used // 4)
        passed = fixed + (places - fixed + offset_by * (used - fixed)) % max(1, amount - fixed)
        return jnp.zeros((amount,), jnp.int32).at[order[jnp.where(places < fixed, places, passed)]].set(jnp.asarray(lengths, jnp.int32))

    lengths = jnp.where(number % 4 == 0, named(crowded, number // 4), named(usual, number - number // 4 - 1))
    mixed = jax.random.permutation(jax.random.fold_in(own, 3), amount)
    source_of, sink = mixed[0:amount // 2 * 2:2], mixed[1:amount // 2 * 2:2]
    margin = jnp.minimum(lengths[source_of] - 1, limit - lengths[sink]) // 2
    margin = jnp.where((source_of == order[0]) | (sink == order[0]) | (lengths[sink] == 0), 0, jnp.maximum(margin, 0))
    passed = jax.random.randint(jax.random.fold_in(own, 4), (amount // 2,), 0, 1 << 20) % (margin + 1)
    lengths = lengths.at[source_of].add(-passed).at[sink].add(passed)
    labels = jnp.searchsorted(jnp.cumsum(lengths), jnp.arange(rows * top), side="right").astype(jnp.int32)
    listing = labels.reshape(top, rows).T
    listing = listing[jax.random.permutation(jax.random.fold_in(own, 1), rows)]
    offset_by = jax.random.randint(jax.random.fold_in(own, 2), (rows, 1), 0, top)
    return jnp.take_along_axis(listing, (jnp.arange(top)[None, :] + offset_by) % top, axis=1)


def shares(number_of, total, most, skew, full):
    portions = [(1 << 20) // math.isqrt(grade ** skew) + 1 for grade in range(1, number_of + 1)]
    largest = most if full else min(most, max(-(-total // number_of), total * portions[0] // sum(portions)))
    least = 1 if total - largest >= number_of - 1 else 0
    given, surplus = [largest] + [least] * (number_of - 1), total - largest - least * (number_of - 1)
    while surplus > 0:
        candidates = [i for i in range(1, number_of) if given[i] < largest] or [i for i in range(1, number_of) if given[i] < most]
        mass, left = sum([portions[i] for i in candidates]), surplus
        for i in candidates:
            extra = min(most - given[i], max(1, left * portions[i] // mass), surplus)
            given[i] = given[i] + extra
            surplus = surplus - extra
    return np.array(given)


def centred(rng, dims, scale, limit, cuts=(), held_as=jnp.bfloat16):
    values = jax.random.normal(rng, dims, jnp.float32) * scale
    if len(cuts) > 0:
        values = levels(rng, dims, cuts, -0.22, 0.18) * values
    return jnp.clip(values, min=-limit, max=limit).astype(held_as)


def setup_inputs(seed: int = 0) -> dict:
    splits = jax.random.split(jax.random.key(seed), 15)
    queries = centred(splits[0], (LANE_TOTAL, STRING_SPAN, HEAD_DIM), 0.09, 0.5, ((0, 64), (1, 8)), jnp.float32)
    key_vectors = draw_key_vectors(jax.random.fold_in(splits[14], 71), 0)
    values = centred(splits[2], (LANE_TOTAL, STRING_SPAN, HEAD_DIM), 1.0, 6.0, ((0, 64), (1, 8)), jnp.float32)
    out_gate = centred(splits[3], (LANE_TOTAL, STRING_SPAN, HEAD_DIM), 1.0, 6.0, ((0, 64), (1, 8)), jnp.float32)
    write_strength = draw_write_strength(jax.random.fold_in(splits[14], 71), 0)
    log_fading_factor = draw_log_fading_factor(jax.random.fold_in(splits[14], 71), 0)
    block_inverse = draw_block_inverse(jax.random.fold_in(splits[14], 71), 0)
    norm_gain = jnp.clip(1.0 + 0.1 * jax.random.normal(splits[7], (HEAD_DIM,), jnp.float32), 0.5, 1.5)
    hidden = centred(splits[8], (TOKENS, D), 1.0, 6.0, ((0, 512),))
    routes_keys = jax.random.split(jax.random.fold_in(splits[9], 1), TOKENS // TOK_DEV)
    routes_turns = jax.random.permutation(jax.random.fold_in(splits[9], 3), TOKENS // TOK_DEV)
    routes = jax.vmap(lambda own, number: assign_block(jax.random.fold_in(splits[9], 2), own, number, TOK_DEV, EXPERTS, TOP, CAP, 2))(routes_keys, routes_turns).reshape((TOKENS, TOP))
    route_weights = jnp.clip(1.0 + 0.18 * jax.random.normal(splits[10], (TOKENS, TOP), jnp.float32), 0.1, 1.9)
    gate_weights = centred(splits[11], (EXPERTS, D, MOE_FF), D ** -0.5, 0.1875, ((0, 512),))
    up_weights = centred(splits[12], (EXPERTS, D, MOE_FF), D ** -0.5, 0.1875, ((0, 512),))
    down_weights = centred(splits[13], (EXPERTS, MOE_FF, D), MOE_FF ** -0.5, 0.25, ((0, 512),))
    return {"queries": queries, "key_vectors": key_vectors, "values": values, "out_gate": out_gate, "write_strength": write_strength, "log_fading_factor": log_fading_factor, "block_inverse": block_inverse, "norm_gain": norm_gain, "hidden": hidden, "routes": routes, "route_weights": route_weights, "gate_weights": gate_weights, "up_weights": up_weights, "down_weights": down_weights}


TOP_PRECISION = lax.Precision.HIGHEST
NORM_EPSILON = 1e-06

def block_parts(queries, key_vectors, values, write_strength, log_fading_factor, block_inverse):
    tracks, length, head_width = queries.shape
    block_size = block_inverse.shape[-1]
    blocks = length // block_size
    shape_four = (tracks, blocks, block_size, head_width)
    query_blocks = queries.reshape(shape_four)
    key_blocks = key_vectors.reshape(shape_four)
    value_blocks = values.reshape(shape_four)
    strength = write_strength.reshape(tracks, blocks, block_size)
    running = jnp.cumsum(log_fading_factor.reshape(tracks, blocks, block_size), axis=-1)
    growth = jnp.exp(running)
    final_log = running[..., -1:]
    write_keys = jnp.einsum('sbij,sbjh->sbih', block_inverse, key_blocks * (strength * growth)[..., None], precision=TOP_PRECISION)
    write_values = jnp.einsum('sbij,sbjh->sbih', block_inverse, value_blocks * strength[..., None], precision=TOP_PRECISION)
    faded_keys = key_blocks * jnp.exp(final_log - running)[..., None]
    faded_queries = query_blocks * growth[..., None]
    row_index = lax.broadcasted_iota(jnp.int32, (block_size, block_size), 0)
    col_index = lax.broadcasted_iota(jnp.int32, (block_size, block_size), 1)
    spread = running[..., :, None] - running[..., None, :]
    causal_fade = jnp.where(row_index >= col_index, jnp.exp(jnp.minimum(spread, 0.0)), 0.0)
    causal = jnp.einsum('sbih,sbjh->sbij', query_blocks, key_blocks, precision=TOP_PRECISION) * causal_fade
    return (faded_queries, write_keys, write_values, faded_keys, causal, jnp.exp(final_log))

def block_step(states, pieces):
    faded_queries, write_keys, write_values, faded_keys, causal, decays = pieces
    fresh_values = write_values - jnp.einsum('sch,shv->scv', write_keys, states, precision=TOP_PRECISION)
    attended = jnp.einsum('sch,shv->scv', faded_queries, states, precision=TOP_PRECISION)
    attended = attended + jnp.einsum('sij,sjv->siv', causal, fresh_values, precision=TOP_PRECISION)
    states = decays[..., None] * states + jnp.einsum('sch,scv->shv', faded_keys, fresh_values, precision=TOP_PRECISION)
    return (states, attended)

def run_blocks(pieces, states):
    moved = tuple((jnp.moveaxis(piece_item, 1, 0) for piece_item in pieces))
    states, attended = lax.scan(block_step, states, moved)
    return (states, jnp.moveaxis(attended, 0, 1))

def gated_norm(attended, norm_gain, out_gate):
    root_mean = jnp.sqrt(lax.optimization_barrier(jnp.mean(attended * attended, axis=-1, keepdims=True)) + NORM_EPSILON)
    return attended / root_mean * norm_gain * jax.nn.silu(out_gate)

def reference(queries, key_vectors, values, out_gate, write_strength, log_fading_factor, block_inverse, norm_gain, hidden, routes, route_weights, gate_weights, up_weights, down_weights):
    tracks, length, head_width = queries.shape
    pieces = block_parts(queries, key_vectors, values, write_strength, log_fading_factor, block_inverse)
    zero_state = jnp.zeros((tracks, head_width, head_width), jnp.float32)
    _, attended = run_blocks(pieces, zero_state)
    mixer_output = gated_norm(attended.reshape(tracks, length, head_width), norm_gain, out_gate)
    pick_list = routes.reshape(-1).astype(jnp.int32)
    by_expert = jnp.argsort(pick_list, stable=True).astype(jnp.int32)
    counts = jnp.zeros((EXPERTS,), jnp.int32).at[pick_list].add(1).astype(jnp.int32)
    starts = (jnp.cumsum(counts) - counts).astype(jnp.int32)
    most_rows = DEVICES * CAP
    padded_order = jnp.concatenate([by_expert, jnp.zeros((most_rows,), jnp.int32)])
    flat_weights = route_weights.reshape(-1)

    def expert_step(summed, expert):
        index_rows = lax.dynamic_slice(padded_order, (starts[expert].astype(jnp.int32),), (most_rows,)).astype(jnp.int32)
        live_rows = jnp.arange(most_rows, dtype=jnp.int32) < counts[expert]
        token_rows = index_rows // TOP
        inputs = hidden[token_rows]
        gate_part = jnp.dot(inputs, gate_weights[expert], preferred_element_type=jnp.float32)
        up_part = jnp.dot(inputs, up_weights[expert], preferred_element_type=jnp.float32)
        active = (jax.nn.silu(gate_part) * up_part).astype(jnp.bfloat16)
        produced = jnp.dot(active, down_weights[expert], preferred_element_type=jnp.float32).astype(jnp.bfloat16)
        produced = lax.optimization_barrier(produced)
        scales = jnp.where(live_rows, flat_weights[index_rows], 0.0)
        summed = summed.at[token_rows].add(produced.astype(jnp.float32) * scales[:, None])
        return (summed, None)
    summed, _ = lax.scan(expert_step, jnp.zeros((TOKENS, D), jnp.float32), jnp.arange(EXPERTS, dtype=jnp.int32))
    expert_output = summed.astype(jnp.bfloat16)
    return (mixer_output, expert_output)
```

```python
import functools

import jax
import jax.numpy as jnp
from jax import lax
from jax.experimental import pallas as pl
from jax.experimental.pallas import tpu as pltpu
from jax.sharding import PartitionSpec as P

TOP_PRECISION = lax.Precision.HIGHEST
NORM_EPSILON = 1e-06
CAPACITY = 3
LANES = 128


def passed_along(block, axis, distance):
    devices = range(lax.axis_size(axis))
    route = [(i - distance, i) for i in devices if i - distance in devices]
    return lax.ppermute(block, axis, route)


def block_parts(queries, key_vectors, values, write_strength, log_fading_factor, block_inverse):
    tracks, length, head_width = queries.shape
    block_size = block_inverse.shape[-1]
    blocks = length // block_size
    shape_four = (tracks, blocks, block_size, head_width)
    query_blocks = queries.reshape(shape_four)
    key_blocks = key_vectors.reshape(shape_four)
    value_blocks = values.reshape(shape_four)
    strength = write_strength.reshape(tracks, blocks, block_size)
    running = jnp.cumsum(log_fading_factor.reshape(tracks, blocks, block_size), axis=-1)
    growth = jnp.exp(running)
    final_log = running[..., -1:]
    write_keys = jnp.einsum(
        "sbij,sbjh->sbih",
        block_inverse,
        key_blocks * (strength * growth)[..., None],
        precision=TOP_PRECISION,
    )
    write_values = jnp.einsum(
        "sbij,sbjh->sbih",
        block_inverse,
        value_blocks * strength[..., None],
        precision=TOP_PRECISION,
    )
    faded_keys = key_blocks * jnp.exp(final_log - running)[..., None]
    faded_queries = query_blocks * growth[..., None]
    row_index = lax.broadcasted_iota(jnp.int32, (block_size, block_size), 0)
    col_index = lax.broadcasted_iota(jnp.int32, (block_size, block_size), 1)
    spread = running[..., :, None] - running[..., None, :]
    causal_fade = jnp.where(row_index >= col_index, jnp.exp(jnp.minimum(spread, 0.0)), 0.0)
    causal = (
        jnp.einsum("sbih,sbjh->sbij", query_blocks, key_blocks, precision=TOP_PRECISION)
        * causal_fade
    )
    return (faded_queries, write_keys, write_values, faded_keys, causal, jnp.exp(final_log))


def block_step(states, pieces):
    faded_queries, write_keys, write_values, faded_keys, causal, decays = pieces
    fresh_values = write_values - jnp.einsum(
        "sch,shv->scv", write_keys, states, precision=TOP_PRECISION
    )
    attended = jnp.einsum("sch,shv->scv", faded_queries, states, precision=TOP_PRECISION)
    attended = attended + jnp.einsum("sij,sjv->siv", causal, fresh_values, precision=TOP_PRECISION)
    states = decays[..., None] * states + jnp.einsum(
        "sch,scv->shv", faded_keys, fresh_values, precision=TOP_PRECISION
    )
    return (states, attended)


def run_blocks(pieces, states):
    moved = tuple((jnp.moveaxis(piece_item, 1, 0) for piece_item in pieces))
    states, attended = lax.scan(block_step, states, moved)
    return (states, jnp.moveaxis(attended, 0, 1))


def gated_norm(attended, norm_gain, out_gate):
    root_mean = jnp.sqrt(jnp.mean(attended * attended, axis=-1, keepdims=True) + NORM_EPSILON)
    return attended / root_mean * norm_gain * jax.nn.silu(out_gate)


def compose(carried, block_piece):
    current_mapping, current_addend = carried
    segment_mapping, segment_addend = block_piece
    updated_mapping = jnp.einsum(
        "qfz,qze->qfe", segment_mapping, current_mapping, precision=TOP_PRECISION
    )
    updated_addend = (
        jnp.einsum("qfz,qze->qfe", segment_mapping, current_addend, precision=TOP_PRECISION)
        + segment_addend
    )
    return ((updated_mapping, updated_addend), None)


def delta_net(
    queries, key_vectors, values, out_gate, write_strength, log_fading_factor, block_inverse, norm_gain
):
    tracks, length, head_width = queries.shape
    pieces = block_parts(
        queries, key_vectors, values, write_strength, log_fading_factor, block_inverse
    )
    faded_queries, write_keys, write_values, faded_keys, causal, decays = pieces
    unit_matrix = jnp.eye(head_width, dtype=jnp.float32)
    identity_map = jnp.broadcast_to(unit_matrix, (tracks, head_width, head_width))
    block_maps = decays[..., None] * unit_matrix - jnp.einsum(
        "sbch,sbck->sbhk", faded_keys, write_keys, precision=TOP_PRECISION
    )
    block_adds = jnp.einsum("sbch,sbcv->sbhv", faded_keys, write_values, precision=TOP_PRECISION)
    (section_mapping, section_addend), _ = lax.scan(
        compose,
        (identity_map, jnp.zeros_like(identity_map)),
        (jnp.moveaxis(block_maps, 1, 0), jnp.moveaxis(block_adds, 1, 0)),
    )
    incoming_state = jnp.zeros_like(section_addend)
    for relay_turn in range(lax.axis_size("ctx") - 1):
        departing_state = (
            jnp.einsum("qfz,qze->qfe", section_mapping, incoming_state, precision=TOP_PRECISION)
            + section_addend
        )
        incoming_state = passed_along(departing_state.astype(jnp.bfloat16), "ctx", 1).astype(
            departing_state.dtype
        )
    _, attended = run_blocks(pieces, incoming_state)
    return gated_norm(attended.reshape(tracks, length, head_width), norm_gain, out_gate)


def named_and_rank(ranks, first, count, tokens):
    row = lax.broadcasted_iota(jnp.int32, (count, tokens), 0) + first
    named = jnp.zeros((count, tokens), jnp.bool_)
    for pick in range(ranks.shape[0]):
        named = jnp.logical_or(named, ranks[pick : pick + 1, :] == row)
    before = lax.broadcasted_iota(jnp.int32, (tokens, tokens), 0) < lax.broadcasted_iota(
        jnp.int32, (tokens, tokens), 1
    )
    earlier = jnp.dot(
        named.astype(jnp.float32).astype(jnp.bfloat16),
        before.astype(jnp.float32).astype(jnp.bfloat16),
        preferred_element_type=jnp.float32,
    )
    return named, earlier


def pack_kernel(ranks_ref, hidden_ref, out_ref, spread_ref):
    tokens, width = hidden_ref.shape
    parts = width // LANES
    per = CAPACITY * parts
    count = out_ref.shape[0] // per
    named, earlier = named_and_rank(
        ranks_ref[...], pl.program_id(0) * count, count, tokens
    )
    for slot in range(CAPACITY):
        chosen = jnp.where(jnp.logical_and(named, earlier == slot), 1.0, 0.0).astype(jnp.bfloat16)
        rows = jnp.dot(chosen, hidden_ref[...], preferred_element_type=jnp.float32)
        for part in range(parts):
            spread_ref[pl.ds(slot * parts + part, count, stride=per), :] = rows[
                :, part * LANES : (part + 1) * LANES
            ]
    out_ref[...] = spread_ref[...].astype(jnp.bfloat16)


def pack_rows(ranks, hidden, experts, steps):
    tokens, width = hidden.shape
    rows = experts * CAPACITY * width // LANES
    return pl.pallas_call(
        pack_kernel,
        grid=(steps,),
        out_shape=jax.ShapeDtypeStruct((rows, LANES), jnp.bfloat16),
        in_specs=[
            pl.BlockSpec(ranks.shape, lambda i: (0, 0)),
            pl.BlockSpec(hidden.shape, lambda i: (0, 0)),
        ],
        out_specs=pl.BlockSpec((rows // steps, LANES), lambda i: (i, 0)),
        scratch_shapes=[pltpu.VMEM((rows // steps, LANES), jnp.float32)],
        compiler_params=pltpu.CompilerParams(vmem_limit_bytes=32 * 1024 * 1024),
        cost_estimate=pl.CostEstimate(
            flops=2 * experts * CAPACITY * tokens * width, bytes_accessed=rows * 256, transcendentals=0
        ),
        name="pack_rows",
    )(ranks, hidden)


def weight_kernel(ranks_ref, weights_ref, high_ref, low_ref):
    tokens = ranks_ref.shape[1]
    experts = high_ref.shape[0] // CAPACITY
    ranks = ranks_ref[...]
    named, earlier = named_and_rank(ranks, 0, experts, tokens)
    row = lax.broadcasted_iota(jnp.int32, (experts, tokens), 0)
    scale = jnp.zeros((experts, tokens), jnp.float32)
    for pick in range(ranks.shape[0]):
        scale = jnp.where(ranks[pick : pick + 1, :] == row, weights_ref[pick : pick + 1, :], scale)
    high = scale.astype(jnp.bfloat16).astype(jnp.float32)
    low = scale - high
    for slot in range(CAPACITY):
        here = jnp.logical_and(named, earlier == slot)
        at = pl.ds(slot * experts, experts)
        high_ref[at, :] = jnp.where(here, high, 0.0).astype(jnp.bfloat16)
        low_ref[at, :] = jnp.where(here, low, 0.0).astype(jnp.bfloat16)


def weight_table(ranks, weights, experts):
    tokens = ranks.shape[1]
    shape = jax.ShapeDtypeStruct((CAPACITY * experts, tokens), jnp.bfloat16)
    return pl.pallas_call(
        weight_kernel,
        out_shape=(shape, shape),
        compiler_params=pltpu.CompilerParams(vmem_limit_bytes=32 * 1024 * 1024),
        cost_estimate=pl.CostEstimate(
            flops=40 * experts * tokens, bytes_accessed=4 * CAPACITY * experts * tokens, transcendentals=0
        ),
        name="weight_table",
    )(ranks, weights)


def expert_kernel(received_ref, gate_ref, up_ref, down_ref, out_ref, spread_ref):
    width = gate_ref.shape[0]
    parts = width // LANES
    per = CAPACITY * parts
    count = received_ref.shape[0] // per
    spread_ref[...] = received_ref[...].astype(jnp.float32)
    rows = jnp.concatenate(
        [
            jnp.concatenate(
                [
                    spread_ref[pl.ds(slot * parts + part, count, stride=per), :].astype(jnp.bfloat16)
                    for part in range(parts)
                ],
                axis=1,
            )
            for slot in range(CAPACITY)
        ],
        axis=0,
    )
    gate = jnp.dot(rows, gate_ref[...], preferred_element_type=jnp.float32)
    up = jnp.dot(rows, up_ref[...], preferred_element_type=jnp.float32)
    active = (gate / (1.0 + jnp.exp(-gate)) * up).astype(jnp.bfloat16)
    produced = jnp.dot(active, down_ref[...], preferred_element_type=jnp.float32)
    for slot in range(CAPACITY):
        for part in range(parts):
            spread_ref[pl.ds(slot * parts + part, count, stride=per), :] = produced[
                slot * count : (slot + 1) * count, part * LANES : (part + 1) * LANES
            ]
    out_ref[...] = spread_ref[...].astype(jnp.bfloat16)


def expert_rows(received, gate_weights, up_weights, down_weights, steps):
    rows = received.shape[0]
    width, units = gate_weights.shape
    slots = rows * LANES // width
    block = pl.BlockSpec((rows // steps, LANES), lambda i: (i, 0))
    return pl.pallas_call(
        expert_kernel,
        grid=(steps,),
        out_shape=jax.ShapeDtypeStruct(received.shape, jnp.bfloat16),
        in_specs=[
            block,
            pl.BlockSpec(gate_weights.shape, lambda i: (0, 0)),
            pl.BlockSpec(up_weights.shape, lambda i: (0, 0)),
            pl.BlockSpec(down_weights.shape, lambda i: (0, 0)),
        ],
        out_specs=block,
        scratch_shapes=[pltpu.VMEM((rows // steps, LANES), jnp.float32)],
        compiler_params=pltpu.CompilerParams(vmem_limit_bytes=40 * 1024 * 1024),
        cost_estimate=pl.CostEstimate(
            flops=6 * slots * width * units,
            bytes_accessed=4 * rows * LANES + 6 * width * units,
            transcendentals=slots * units,
        ),
        name="expert_rows",
    )(received, gate_weights, up_weights, down_weights)


def combine_kernel(returned_ref, high_ref, low_ref, out_ref, spread_ref):
    tokens, width = out_ref.shape
    parts = width // LANES
    per = CAPACITY * parts
    count = returned_ref.shape[0] // per
    spread_ref[...] = returned_ref[...].astype(jnp.float32)
    total = jnp.zeros((tokens, width), jnp.float32)
    for slot in range(CAPACITY):
        rows = jnp.concatenate(
            [
                spread_ref[pl.ds(slot * parts + part, count, stride=per), :].astype(jnp.bfloat16)
                for part in range(parts)
            ],
            axis=1,
        )
        at = pl.ds(slot * count, count)
        for table in (high_ref, low_ref):
            total = total + lax.dot_general(
                table[at, :], rows, (((0,), (0,)), ((), ())), preferred_element_type=jnp.float32
            )
    out_ref[...] = total.astype(jnp.bfloat16)


def combine_rows(returned, high, low, tokens, width):
    rows = returned.shape[0]
    return pl.pallas_call(
        combine_kernel,
        out_shape=jax.ShapeDtypeStruct((tokens, width), jnp.bfloat16),
        scratch_shapes=[pltpu.VMEM((rows, LANES), jnp.float32)],
        compiler_params=pltpu.CompilerParams(vmem_limit_bytes=48 * 1024 * 1024),
        cost_estimate=pl.CostEstimate(
            flops=4 * rows * LANES * tokens, bytes_accessed=2 * rows * LANES, transcendentals=0
        ),
        name="combine_rows",
    )(returned, high, low)


def exchange(rows):
    return lax.all_to_all(rows, ("exp", "ctx"), split_axis=0, concat_axis=0, tiled=True)


def body(
    queries,
    key_vectors,
    values,
    out_gate,
    write_strength,
    log_fading_factor,
    block_inverse,
    norm_gain,
    hidden,
    routes,
    route_weights,
    gate_weights,
    up_weights,
    down_weights,
):
    tokens, width = hidden.shape
    context_size = lax.axis_size("ctx")
    owner_count = lax.axis_size("exp")
    experts = context_size * owner_count
    ranks = (routes % owner_count * context_size + routes // owner_count).T
    outgoing = pack_rows(ranks, hidden, experts, 4)
    received = exchange(outgoing)
    produced = expert_rows(received, gate_weights[0], up_weights[0], down_weights[0], 4)
    returned = exchange(produced)
    high, low = weight_table(ranks, route_weights.T, experts)
    expert_output = combine_rows(returned, high, low, tokens, width)
    mixer_output = delta_net(
        queries, key_vectors, values, out_gate, write_strength, log_fading_factor, block_inverse, norm_gain
    )
    return (mixer_output, expert_output)


def solution(mesh):
    placed = (
        P("exp", "ctx", None),
        P("exp", "ctx", None),
        P("exp", "ctx", None),
        P("exp", "ctx", None),
        P("exp", "ctx"),
        P("exp", "ctx"),
        P("exp", "ctx", None, None),
        P(),
        P(("ctx", "exp"), None),
        P(("ctx", "exp"), None),
        P(("ctx", "exp"), None),
        P(("ctx", "exp"), None, None),
        P(("ctx", "exp"), None, None),
        P(("ctx", "exp"), None, None),
    )
    return jax.shard_map(
        body,
        mesh=mesh,
        in_specs=placed,
        out_specs=(P("exp", "ctx", None), P(("ctx", "exp"), None)),
        check_vma=False,
    )
```

```python
import functools

import jax
import jax.numpy as jnp
from jax import lax
from jax.experimental import pallas as pl
from jax.experimental.pallas import tpu as pltpu
from jax.sharding import PartitionSpec as P

TOP_PRECISION = lax.Precision.HIGHEST
NORM_EPSILON = 1e-06
CAPACITY = 3
LANES = 128
VMEM_BYTES = 60 * 1024 * 1024


def passed_along(block, axis, distance):
    devices = range(lax.axis_size(axis))
    route = [(i - distance, i) for i in devices if i - distance in devices]
    return lax.ppermute(block, axis, route)


def block_parts(queries, key_vectors, values, write_strength, log_fading_factor, block_inverse):
    tracks, length, head_width = queries.shape
    block_size = block_inverse.shape[-1]
    blocks = length // block_size
    shape_four = (tracks, blocks, block_size, head_width)
    query_blocks = queries.reshape(shape_four)
    key_blocks = key_vectors.reshape(shape_four)
    value_blocks = values.reshape(shape_four)
    strength = write_strength.reshape(tracks, blocks, block_size)
    running = jnp.cumsum(log_fading_factor.reshape(tracks, blocks, block_size), axis=-1)
    growth = jnp.exp(running)
    final_log = running[..., -1:]
    write_keys = jnp.einsum(
        "sbij,sbjh->sbih",
        block_inverse,
        key_blocks * (strength * growth)[..., None],
        precision=TOP_PRECISION,
    )
    write_values = jnp.einsum(
        "sbij,sbjh->sbih",
        block_inverse,
        value_blocks * strength[..., None],
        precision=TOP_PRECISION,
    )
    faded_keys = key_blocks * jnp.exp(final_log - running)[..., None]
    faded_queries = query_blocks * growth[..., None]
    row_index = lax.broadcasted_iota(jnp.int32, (block_size, block_size), 0)
    col_index = lax.broadcasted_iota(jnp.int32, (block_size, block_size), 1)
    spread = running[..., :, None] - running[..., None, :]
    causal_fade = jnp.where(row_index >= col_index, jnp.exp(jnp.minimum(spread, 0.0)), 0.0)
    causal = (
        jnp.einsum("sbih,sbjh->sbij", query_blocks, key_blocks, precision=TOP_PRECISION)
        * causal_fade
    )
    return (faded_queries, write_keys, write_values, faded_keys, causal, jnp.exp(final_log))


def block_step(states, pieces):
    faded_queries, write_keys, write_values, faded_keys, causal, decays = pieces
    fresh_values = write_values - jnp.einsum(
        "sch,shv->scv", write_keys, states, precision=TOP_PRECISION
    )
    attended = jnp.einsum("sch,shv->scv", faded_queries, states, precision=TOP_PRECISION)
    attended = attended + jnp.einsum("sij,sjv->siv", causal, fresh_values, precision=TOP_PRECISION)
    states = decays[..., None] * states + jnp.einsum(
        "sch,scv->shv", faded_keys, fresh_values, precision=TOP_PRECISION
    )
    return (states, attended)


def run_blocks(pieces, states):
    moved = tuple((jnp.moveaxis(piece_item, 1, 0) for piece_item in pieces))
    states, attended = lax.scan(block_step, states, moved)
    return (states, jnp.moveaxis(attended, 0, 1))


def gated_norm(attended, norm_gain, out_gate):
    root_mean = jnp.sqrt(jnp.mean(attended * attended, axis=-1, keepdims=True) + NORM_EPSILON)
    return attended / root_mean * norm_gain * jax.nn.silu(out_gate)


def compose(carried, block_piece):
    current_mapping, current_addend = carried
    segment_mapping, segment_addend = block_piece
    updated_mapping = jnp.einsum(
        "qfz,qze->qfe", segment_mapping, current_mapping, precision=TOP_PRECISION
    )
    updated_addend = (
        jnp.einsum("qfz,qze->qfe", segment_mapping, current_addend, precision=TOP_PRECISION)
        + segment_addend
    )
    return ((updated_mapping, updated_addend), None)


def delta_front(queries, key_vectors, values, write_strength, log_fading_factor, block_inverse):
    tracks, length, head_width = queries.shape
    pieces = block_parts(
        queries, key_vectors, values, write_strength, log_fading_factor, block_inverse
    )
    faded_queries, write_keys, write_values, faded_keys, causal, decays = pieces
    unit_matrix = jnp.eye(head_width, dtype=jnp.float32)
    identity_map = jnp.broadcast_to(unit_matrix, (tracks, head_width, head_width))
    block_maps = decays[..., None] * unit_matrix - jnp.einsum(
        "sbch,sbck->sbhk", faded_keys, write_keys, precision=TOP_PRECISION
    )
    block_adds = jnp.einsum("sbch,sbcv->sbhv", faded_keys, write_values, precision=TOP_PRECISION)
    (section_mapping, section_addend), _ = lax.scan(
        compose,
        (identity_map, jnp.zeros_like(identity_map)),
        (jnp.moveaxis(block_maps, 1, 0), jnp.moveaxis(block_adds, 1, 0)),
    )
    incoming_state = jnp.zeros_like(section_addend)
    for relay_turn in range(lax.axis_size("ctx") - 1):
        departing_state = (
            jnp.einsum("qfz,qze->qfe", section_mapping, incoming_state, precision=TOP_PRECISION)
            + section_addend
        )
        incoming_state = passed_along(departing_state.astype(jnp.bfloat16), "ctx", 1).astype(
            departing_state.dtype
        )
    return pieces, incoming_state


def named_and_rank(ranks, first, count, tokens):
    row = lax.broadcasted_iota(jnp.int32, (count, tokens), 0) + first
    named = jnp.zeros((count, tokens), jnp.bool_)
    for pick in range(ranks.shape[0]):
        named = jnp.logical_or(named, ranks[pick : pick + 1, :] == row)
    before = lax.broadcasted_iota(jnp.int32, (tokens, tokens), 0) < lax.broadcasted_iota(
        jnp.int32, (tokens, tokens), 1
    )
    earlier = jnp.dot(
        named.astype(jnp.float32).astype(jnp.bfloat16),
        before.astype(jnp.float32).astype(jnp.bfloat16),
        preferred_element_type=jnp.float32,
    )
    return named, earlier


def pack_kernel(owner_count, context_size, routes_ref, hidden_ref, out_ref, spread_ref):
    tokens, width = hidden_ref.shape
    parts = width // LANES
    per = CAPACITY * parts
    count = out_ref.shape[0] // per
    routes = routes_ref[...].astype(jnp.float32)
    context = jnp.floor(routes * (1.0 / owner_count))
    pieces = (context, routes - context * owner_count)
    diagonal = (
        lax.broadcasted_iota(jnp.int32, (tokens, tokens), 0)
        == lax.broadcasted_iota(jnp.int32, (tokens, tokens), 1)
    )
    unit = diagonal.astype(jnp.float32).astype(jnp.bfloat16)
    context, owner = (
        lax.dot_general(
            piece.astype(jnp.bfloat16),
            unit,
            (((0,), (0,)), ((), ())),
            preferred_element_type=jnp.float32,
        )
        for piece in pieces
    )
    ranks = (owner * context_size + context).astype(jnp.int32)
    named, earlier = named_and_rank(ranks, pl.program_id(0) * count, count, tokens)
    for slot in range(CAPACITY):
        chosen = jnp.where(jnp.logical_and(named, earlier == slot), 1.0, 0.0).astype(jnp.bfloat16)
        rows = jnp.dot(chosen, hidden_ref[...], preferred_element_type=jnp.float32)
        for part in range(parts):
            spread_ref[pl.ds(slot * parts + part, count, stride=per), :] = rows[
                :, part * LANES : (part + 1) * LANES
            ]
    out_ref[...] = spread_ref[...].astype(jnp.bfloat16)


def pack_rows(routes, hidden, owner_count, context_size, steps):
    tokens, width = hidden.shape
    experts = owner_count * context_size
    rows = experts * CAPACITY * width // LANES
    return pl.pallas_call(
        functools.partial(pack_kernel, owner_count, context_size),
        grid=(steps,),
        out_shape=jax.ShapeDtypeStruct((rows, LANES), jnp.bfloat16),
        in_specs=[
            pl.BlockSpec(routes.shape, lambda i: (0, 0)),
            pl.BlockSpec(hidden.shape, lambda i: (0, 0)),
        ],
        out_specs=pl.BlockSpec((rows // steps, LANES), lambda i: (i, 0)),
        scratch_shapes=[pltpu.VMEM((rows // steps, LANES), jnp.float32)],
        compiler_params=pltpu.CompilerParams(vmem_limit_bytes=VMEM_BYTES),
        cost_estimate=pl.CostEstimate(
            flops=2 * experts * CAPACITY * tokens * width, bytes_accessed=rows * 256, transcendentals=0
        ),
        name="pack_rows",
    )(routes, hidden)


def weight_kernel(ranks_ref, weights_ref, high_ref, low_ref):
    tokens = ranks_ref.shape[1]
    experts = high_ref.shape[1]
    ranks = ranks_ref[...]
    named, earlier = named_and_rank(ranks, 0, experts, tokens)
    row = lax.broadcasted_iota(jnp.int32, (experts, tokens), 0)
    scale = jnp.zeros((experts, tokens), jnp.float32)
    for pick in range(ranks.shape[0]):
        scale = jnp.where(ranks[pick : pick + 1, :] == row, weights_ref[pick : pick + 1, :], scale)
    high = scale.astype(jnp.bfloat16).astype(jnp.float32)
    low = scale - high
    for slot in range(CAPACITY):
        here = jnp.logical_and(named, earlier == slot)
        high_ref[slot] = jnp.where(here, high, 0.0).astype(jnp.bfloat16)
        low_ref[slot] = jnp.where(here, low, 0.0).astype(jnp.bfloat16)


def weight_table(ranks, weights, experts):
    tokens = ranks.shape[1]
    shape = jax.ShapeDtypeStruct((CAPACITY, experts, tokens), jnp.bfloat16)
    return pl.pallas_call(
        weight_kernel,
        out_shape=(shape, shape),
        compiler_params=pltpu.CompilerParams(vmem_limit_bytes=32 * 1024 * 1024),
        cost_estimate=pl.CostEstimate(
            flops=40 * experts * tokens, bytes_accessed=4 * CAPACITY * experts * tokens, transcendentals=0
        ),
        name="weight_table",
    )(ranks, weights)


def expert_kernel(
    received_ref, gate_ref, up_ref, down_ref, out_ref, spread_ref, gate_here, up_here, down_here, ready
):
    width = gate_here.shape[0]
    parts = width // LANES
    per = CAPACITY * parts
    count = received_ref.shape[0] // per
    loads = [
        pltpu.make_async_copy(there, here, ready.at[i])
        for i, (there, here) in enumerate(
            ((gate_ref, gate_here), (up_ref, up_here), (down_ref, down_here))
        )
    ]
    first = pl.program_id(0) == 0

    @pl.when(first)
    def _():
        for load in loads:
            load.start()

    spread_ref[...] = received_ref[...].astype(jnp.float32)
    rows = jnp.concatenate(
        [
            jnp.concatenate(
                [
                    spread_ref[pl.ds(slot * parts + part, count, stride=per), :].astype(jnp.bfloat16)
                    for part in range(parts)
                ],
                axis=1,
            )
            for slot in range(CAPACITY)
        ],
        axis=0,
    )

    @pl.when(first)
    def _():
        for load in loads:
            load.wait()

    gate = jnp.dot(rows, gate_here[...], preferred_element_type=jnp.float32)
    up = jnp.dot(rows, up_here[...], preferred_element_type=jnp.float32)
    active = (gate / (1.0 + jnp.exp(-gate)) * up).astype(jnp.bfloat16)
    produced = jnp.dot(active, down_here[...], preferred_element_type=jnp.float32)
    for slot in range(CAPACITY):
        for part in range(parts):
            spread_ref[pl.ds(slot * parts + part, count, stride=per), :] = produced[
                slot * count : (slot + 1) * count, part * LANES : (part + 1) * LANES
            ]
    out_ref[...] = spread_ref[...].astype(jnp.bfloat16)


def expert_rows(received, gate_weights, up_weights, down_weights, steps):
    rows = received.shape[0]
    width, units = gate_weights.shape
    slots = rows * LANES // width
    block = pl.BlockSpec((rows // steps, LANES), lambda i: (i, 0))
    whole = pl.BlockSpec(memory_space=pl.ANY)
    return pl.pallas_call(
        expert_kernel,
        grid=(steps,),
        out_shape=jax.ShapeDtypeStruct(received.shape, jnp.bfloat16),
        in_specs=[block, whole, whole, whole],
        out_specs=block,
        scratch_shapes=[
            pltpu.VMEM((rows // steps, LANES), jnp.float32),
            pltpu.VMEM(gate_weights.shape, jnp.bfloat16),
            pltpu.VMEM(up_weights.shape, jnp.bfloat16),
            pltpu.VMEM(down_weights.shape, jnp.bfloat16),
            pltpu.SemaphoreType.DMA((3,)),
        ],
        compiler_params=pltpu.CompilerParams(vmem_limit_bytes=VMEM_BYTES),
        cost_estimate=pl.CostEstimate(
            flops=6 * slots * width * units,
            bytes_accessed=4 * rows * LANES + 6 * width * units,
            transcendentals=slots * units,
        ),
        name="expert_rows",
    )(received, gate_weights, up_weights, down_weights)


def combine_kernel(returned_ref, high_ref, low_ref, out_ref, spread_ref, total_ref):
    tokens, width = out_ref.shape
    parts = width // LANES
    per = CAPACITY * parts
    count = returned_ref.shape[0] // per
    step = pl.program_id(0)

    @pl.when(step == 0)
    def _():
        total_ref[...] = jnp.zeros_like(total_ref)

    spread_ref[...] = returned_ref[...].astype(jnp.float32)
    total = total_ref[...]
    for slot in range(CAPACITY):
        rows = jnp.concatenate(
            [
                spread_ref[pl.ds(slot * parts + part, count, stride=per), :].astype(jnp.bfloat16)
                for part in range(parts)
            ],
            axis=1,
        )
        for table in (high_ref, low_ref):
            total = total + lax.dot_general(
                table[slot], rows, (((0,), (0,)), ((), ())), preferred_element_type=jnp.float32
            )
    total_ref[...] = total

    @pl.when(step == pl.num_programs(0) - 1)
    def _():
        out_ref[...] = total.astype(jnp.bfloat16)


def combine_rows(returned, high, low, tokens, width, steps):
    rows = returned.shape[0]
    experts = high.shape[1]
    table = pl.BlockSpec((CAPACITY, experts // steps, tokens), lambda i: (0, i, 0))
    return pl.pallas_call(
        combine_kernel,
        grid=(steps,),
        out_shape=jax.ShapeDtypeStruct((tokens, width), jnp.bfloat16),
        in_specs=[pl.BlockSpec((rows // steps, LANES), lambda i: (i, 0)), table, table],
        out_specs=pl.BlockSpec((tokens, width), lambda i: (0, 0)),
        scratch_shapes=[
            pltpu.VMEM((rows // steps, LANES), jnp.float32),
            pltpu.VMEM((tokens, width), jnp.float32),
        ],
        compiler_params=pltpu.CompilerParams(vmem_limit_bytes=VMEM_BYTES),
        cost_estimate=pl.CostEstimate(
            flops=4 * rows * LANES * tokens, bytes_accessed=2 * rows * LANES, transcendentals=0
        ),
        name="combine_rows",
    )(returned, high, low)


def exchange(rows):
    return lax.all_to_all(rows, ("exp", "ctx"), split_axis=0, concat_axis=0, tiled=True)


def body(
    queries,
    key_vectors,
    values,
    out_gate,
    write_strength,
    log_fading_factor,
    block_inverse,
    norm_gain,
    hidden,
    routes,
    route_weights,
    gate_weights,
    up_weights,
    down_weights,
):
    tokens, width = hidden.shape
    context_size = lax.axis_size("ctx")
    owner_count = lax.axis_size("exp")
    experts = context_size * owner_count
    outgoing = pack_rows(routes, hidden, owner_count, context_size, 4)
    received = exchange(outgoing)
    pieces, incoming_state = delta_front(
        queries, key_vectors, values, write_strength, log_fading_factor, block_inverse
    )
    received, incoming_state = lax.optimization_barrier((received, incoming_state))
    produced = expert_rows(received, gate_weights[0], up_weights[0], down_weights[0], 4)
    returned = exchange(produced)
    ranks = (routes % owner_count * context_size + routes // owner_count).T
    high, low = weight_table(ranks, route_weights.T, experts)
    expert_output = combine_rows(returned, high, low, tokens, width, 4)
    _, attended = run_blocks(pieces, incoming_state)
    mixer_output = gated_norm(attended.reshape(out_gate.shape), norm_gain, out_gate)
    return (mixer_output, expert_output)


def solution(mesh):
    placed = (
        P("exp", "ctx", None),
        P("exp", "ctx", None),
        P("exp", "ctx", None),
        P("exp", "ctx", None),
        P("exp", "ctx"),
        P("exp", "ctx"),
        P("exp", "ctx", None, None),
        P(),
        P(("ctx", "exp"), None),
        P(("ctx", "exp"), None),
        P(("ctx", "exp"), None),
        P(("ctx", "exp"), None, None),
        P(("ctx", "exp"), None, None),
        P(("ctx", "exp"), None, None),
    )
    return jax.shard_map(
        body,
        mesh=mesh,
        in_specs=placed,
        out_specs=(P("exp", "ctx", None), P(("ctx", "exp"), None)),
        check_vma=False,
    )
```

```python
import functools
import math

import jax
import jax.numpy as jnp
from jax import lax
from jax.experimental import pallas as pl
from jax.experimental.pallas import tpu as pltpu
from jax.sharding import PartitionSpec as P

TOP_PRECISION = lax.Precision.HIGHEST
NORM_EPSILON = 1e-06
CAPACITY = 3
CORES = 2
LANES = 128
META_ROWS = 16
VMEM_BYTES = 60 * 1024 * 1024


def passed_along(block, axis, distance):
    devices = range(lax.axis_size(axis))
    route = [(i - distance, i) for i in devices if i - distance in devices]
    return lax.ppermute(block, axis, route)


def block_parts(queries, key_vectors, values, write_strength, log_fading_factor, block_inverse):
    tracks, length, head_width = queries.shape
    block_size = block_inverse.shape[-1]
    blocks = length // block_size
    shape_four = (tracks, blocks, block_size, head_width)
    query_blocks = queries.reshape(shape_four)
    key_blocks = key_vectors.reshape(shape_four)
    value_blocks = values.reshape(shape_four)
    strength = write_strength.reshape(tracks, blocks, block_size)
    running = jnp.cumsum(log_fading_factor.reshape(tracks, blocks, block_size), axis=-1)
    growth = jnp.exp(running)
    final_log = running[..., -1:]
    write_keys = jnp.einsum(
        "sbij,sbjh->sbih",
        block_inverse,
        key_blocks * (strength * growth)[..., None],
        precision=TOP_PRECISION,
    )
    write_values = jnp.einsum(
        "sbij,sbjh->sbih",
        block_inverse,
        value_blocks * strength[..., None],
        precision=TOP_PRECISION,
    )
    faded_keys = key_blocks * jnp.exp(final_log - running)[..., None]
    faded_queries = query_blocks * growth[..., None]
    row_index = lax.broadcasted_iota(jnp.int32, (block_size, block_size), 0)
    col_index = lax.broadcasted_iota(jnp.int32, (block_size, block_size), 1)
    spread = running[..., :, None] - running[..., None, :]
    causal_fade = jnp.where(row_index >= col_index, jnp.exp(jnp.minimum(spread, 0.0)), 0.0)
    causal = (
        jnp.einsum("sbih,sbjh->sbij", query_blocks, key_blocks, precision=TOP_PRECISION)
        * causal_fade
    )
    return (faded_queries, write_keys, write_values, faded_keys, causal, jnp.exp(final_log))


def block_step(states, pieces):
    faded_queries, write_keys, write_values, faded_keys, causal, decays = pieces
    fresh_values = write_values - jnp.einsum(
        "sch,shv->scv", write_keys, states, precision=TOP_PRECISION
    )
    attended = jnp.einsum("sch,shv->scv", faded_queries, states, precision=TOP_PRECISION)
    attended = attended + jnp.einsum("sij,sjv->siv", causal, fresh_values, precision=TOP_PRECISION)
    states = decays[..., None] * states + jnp.einsum(
        "sch,scv->shv", faded_keys, fresh_values, precision=TOP_PRECISION
    )
    return (states, attended)


def run_blocks(pieces, states):
    moved = tuple((jnp.moveaxis(piece_item, 1, 0) for piece_item in pieces))
    states, attended = lax.scan(block_step, states, moved)
    return (states, jnp.moveaxis(attended, 0, 1))


def gated_norm(attended, norm_gain, out_gate):
    root_mean = jnp.sqrt(jnp.mean(attended * attended, axis=-1, keepdims=True) + NORM_EPSILON)
    return attended / root_mean * norm_gain * jax.nn.silu(out_gate)


def compose(carried, block_piece):
    current_mapping, current_addend = carried
    segment_mapping, segment_addend = block_piece
    updated_mapping = jnp.einsum(
        "qfz,qze->qfe", segment_mapping, current_mapping, precision=TOP_PRECISION
    )
    updated_addend = (
        jnp.einsum("qfz,qze->qfe", segment_mapping, current_addend, precision=TOP_PRECISION)
        + segment_addend
    )
    return ((updated_mapping, updated_addend), None)


def delta_front(queries, key_vectors, values, write_strength, log_fading_factor, block_inverse):
    tracks, length, head_width = queries.shape
    pieces = block_parts(
        queries, key_vectors, values, write_strength, log_fading_factor, block_inverse
    )
    faded_queries, write_keys, write_values, faded_keys, causal, decays = pieces
    unit_matrix = jnp.eye(head_width, dtype=jnp.float32)
    identity_map = jnp.broadcast_to(unit_matrix, (tracks, head_width, head_width))
    block_maps = decays[..., None] * unit_matrix - jnp.einsum(
        "sbch,sbck->sbhk", faded_keys, write_keys, precision=TOP_PRECISION
    )
    block_adds = jnp.einsum("sbch,sbcv->sbhv", faded_keys, write_values, precision=TOP_PRECISION)
    (section_mapping, section_addend), _ = lax.scan(
        compose,
        (identity_map, jnp.zeros_like(identity_map)),
        (jnp.moveaxis(block_maps, 1, 0), jnp.moveaxis(block_adds, 1, 0)),
    )
    incoming_state = jnp.zeros_like(section_addend)
    for relay_turn in range(lax.axis_size("ctx") - 1):
        departing_state = (
            jnp.einsum("qfz,qze->qfe", section_mapping, incoming_state, precision=TOP_PRECISION)
            + section_addend
        )
        incoming_state = passed_along(departing_state.astype(jnp.bfloat16), "ctx", 1).astype(
            departing_state.dtype
        )
    return pieces, incoming_state


def device_of(x, core, y, z, side):
    return ((x * CORES + core) * side + y) * side + z


def line_groups(chips, side):
    first = [[device_of(x, 0, y, z, side) for y in range(side)] for x in range(chips) for z in range(side)]
    second = [[device_of(x, 1, y, z, side) for z in range(side)] for x in range(chips) for y in range(side)]
    return first + second


def plane_groups(chips, side):
    first = [[device_of(x, 0, y, z, side) for x in range(chips) for z in range(side)] for y in range(side)]
    second = [[device_of(x, 1, y, z, side) for x in range(chips) for y in range(side)] for z in range(side)]
    return first + second


def exchange(rows, groups):
    return lax.all_to_all(
        rows, ("ctx", "exp"), split_axis=0, concat_axis=0, tiled=True, axis_index_groups=groups
    )


def head_kernel(experts, picks_ref, line_ref, place_ref, weights_ref, hidden_ref, out_ref, block_ref):
    tokens = hidden_ref.shape[0]
    top = picks_ref.shape[0]

    @pl.when(pl.program_id(0) == 0)
    def _():
        picks = picks_ref[...]
        row = lax.broadcasted_iota(jnp.int32, (experts, tokens), 0)
        named = jnp.zeros((experts, tokens), jnp.bool_)
        for pick in range(top):
            named = jnp.logical_or(named, picks[pick : pick + 1, :] == row)
        before = lax.broadcasted_iota(jnp.int32, (tokens, tokens), 0) < lax.broadcasted_iota(
            jnp.int32, (tokens, tokens), 1
        )
        earlier = jnp.dot(
            named.astype(jnp.float32).astype(jnp.bfloat16),
            before.astype(jnp.float32).astype(jnp.bfloat16),
            preferred_element_type=jnp.float32,
        )
        slot = jnp.concatenate(
            [
                jnp.sum(
                    jnp.where(picks[pick : pick + 1, :] == row, earlier, 0.0), axis=0, keepdims=True
                )
                for pick in range(top)
            ],
            axis=0,
        )
        weights = weights_ref[...]
        high = weights.astype(jnp.bfloat16).astype(jnp.float32)
        block_ref[...] = jnp.zeros_like(block_ref)
        block_ref[0:tokens, :] = hidden_ref[...].astype(jnp.float32)
        for column, item in enumerate(
            (line_ref[...], place_ref[0] + slot * place_ref[1], high, weights - high)
        ):
            block_ref[tokens : tokens + top, column * tokens : (column + 1) * tokens] = item

    out_ref[...] = block_ref[...].astype(jnp.bfloat16)


def head_rows(picks, line, place, weights, hidden, experts, copies):
    tokens, width = hidden.shape
    shape = (tokens + META_ROWS, width)
    return pl.pallas_call(
        functools.partial(head_kernel, experts),
        grid=(copies,),
        out_shape=jax.ShapeDtypeStruct((copies * shape[0], width), jnp.bfloat16),
        in_specs=[
            pl.BlockSpec(picks.shape, lambda i: (0, 0)),
            pl.BlockSpec(line.shape, lambda i: (0, 0)),
            pl.BlockSpec(place.shape, lambda i: (0, 0, 0)),
            pl.BlockSpec(weights.shape, lambda i: (0, 0)),
            pl.BlockSpec(hidden.shape, lambda i: (0, 0)),
        ],
        out_specs=pl.BlockSpec(shape, lambda i: (i, 0)),
        scratch_shapes=[pltpu.VMEM(shape, jnp.float32)],
        compiler_params=pltpu.CompilerParams(vmem_limit_bytes=VMEM_BYTES),
        cost_estimate=pl.CostEstimate(
            flops=2 * experts * tokens * tokens, bytes_accessed=2 * copies * shape[0] * width, transcendentals=0
        ),
        name="head_rows",
    )(picks, line, place, weights, hidden)


def table_at(meta, mine, count, value):
    tokens = value.shape[1]
    row = lax.broadcasted_iota(jnp.int32, (count, tokens), 0).astype(jnp.float32)
    place = jnp.where(meta[:, 0:tokens] == mine, meta[:, tokens : 2 * tokens], -1.0)
    table = jnp.zeros((count, tokens), jnp.float32)
    for pick in range(value.shape[0]):
        table = jnp.where(place[pick : pick + 1, :] == row, value[pick : pick + 1, :], table)
    return table


def pack_kernel(top, mine_ref, meta_ref, data_ref, out_ref, table_ref, spread_ref):
    sources, tokens, _ = data_ref.shape
    count = table_ref.shape[1]
    near = count // CAPACITY
    lanes = spread_ref.shape[2]

    @pl.when(pl.program_id(0) == 0)
    def _():
        mine = mine_ref[0].astype(jnp.float32)
        for source in range(sources):
            meta = meta_ref[source].astype(jnp.float32)[0:top]
            ones = jnp.ones((top, tokens), jnp.float32)
            table_ref[source] = table_at(meta, mine, count, ones).astype(jnp.bfloat16)

    for source in range(sources):
        rows = jnp.dot(table_ref[source], data_ref[source], preferred_element_type=jnp.float32)
        for slot in range(CAPACITY):
            at = pl.ds(slot * sources + source, near, stride=CAPACITY * sources)
            for part in range(spread_ref.shape[0]):
                spread_ref[part, at, :] = rows[
                    slot * near : (slot + 1) * near, part * lanes : (part + 1) * lanes
                ]
    for part in range(spread_ref.shape[0]):
        out_ref[:, part * lanes : (part + 1) * lanes] = spread_ref[part].astype(jnp.bfloat16)


def pack_rows(mine, gathered, tokens, top, near, columns):
    sources, _, width = gathered.shape
    rows = near * CAPACITY * sources
    return pl.pallas_call(
        functools.partial(pack_kernel, top),
        grid=(width // columns,),
        out_shape=jax.ShapeDtypeStruct((rows, width), jnp.bfloat16),
        in_specs=[
            pl.BlockSpec(memory_space=pltpu.SMEM),
            pl.BlockSpec((sources, META_ROWS, 4 * tokens), lambda i: (0, tokens // META_ROWS, 0)),
            pl.BlockSpec((sources, tokens, columns), lambda i: (0, 0, i)),
        ],
        out_specs=pl.BlockSpec((rows, columns), lambda i: (0, i)),
        scratch_shapes=[
            pltpu.VMEM((sources, near * CAPACITY, tokens), jnp.bfloat16),
            pltpu.VMEM((columns // LANES, rows, LANES), jnp.float32),
        ],
        compiler_params=pltpu.CompilerParams(vmem_limit_bytes=VMEM_BYTES),
        cost_estimate=pl.CostEstimate(
            flops=2 * rows * tokens * width, bytes_accessed=4 * rows * width, transcendentals=0
        ),
        name="pack_rows",
    )(mine, gathered, gathered)


def expert_kernel(received_ref, *refs):
    weight_refs, out_ref, here = refs[:6], refs[6], refs[7:13]
    spread_ref, ready = refs[13:]
    loads = [
        pltpu.make_async_copy(there, place, ready.at[i])
        for i, (there, place) in enumerate(zip(weight_refs, here))
    ]
    first = pl.program_id(0) == 0

    @pl.when(first)
    def _():
        for load in loads:
            load.start()

    senders, each, width = spread_ref.shape
    half = each // CORES
    spread_ref[...] = received_ref[...].astype(jnp.float32).reshape(spread_ref.shape)
    for turn in range(CORES):
        at = pl.ds(turn * half, half)
        rows = spread_ref[:, at, :].reshape(senders * half, width).astype(jnp.bfloat16)

        @pl.when(first)
        def _():
            for load in loads[3 * turn : 3 * turn + 3]:
                load.wait()

        gate_here, up_here, down_here = here[3 * turn : 3 * turn + 3]
        gate = jnp.dot(rows, gate_here[...], preferred_element_type=jnp.float32)
        up = jnp.dot(rows, up_here[...], preferred_element_type=jnp.float32)
        active = (gate / (1.0 + jnp.exp(-gate)) * up).astype(jnp.bfloat16)
        produced = jnp.dot(active, down_here[...], preferred_element_type=jnp.float32)
        spread_ref[:, at, :] = produced.reshape(senders, half, width)
    out_ref[...] = spread_ref[...].reshape(out_ref.shape).astype(jnp.bfloat16)


def expert_rows(received, weights, senders, steps):
    rows, width = received.shape
    units = weights[0].shape[1]
    block = pl.BlockSpec((rows // steps, width), lambda i: (i, 0))
    whole = pl.BlockSpec(memory_space=pl.ANY)
    return pl.pallas_call(
        expert_kernel,
        grid=(steps,),
        out_shape=jax.ShapeDtypeStruct(received.shape, jnp.bfloat16),
        in_specs=[block] + [whole] * len(weights),
        out_specs=block,
        scratch_shapes=[pltpu.VMEM(weight.shape, jnp.bfloat16) for weight in weights]
        + [
            pltpu.VMEM((senders // steps, rows // senders, width), jnp.float32),
            pltpu.SemaphoreType.DMA((len(weights),)),
        ],
        compiler_params=pltpu.CompilerParams(vmem_limit_bytes=VMEM_BYTES),
        cost_estimate=pl.CostEstimate(
            flops=6 * rows * width * units,
            bytes_accessed=4 * rows * width + 12 * width * units,
            transcendentals=rows * units,
        ),
        name="expert_rows",
    )(received, *weights)


def combine_kernel(top, mine_ref, meta_ref, returned_ref, out_ref, high_ref, low_ref, spread_ref):
    sources, tokens, _ = out_ref.shape
    count = high_ref.shape[1]
    near = count // CAPACITY
    lanes = spread_ref.shape[2]

    @pl.when(pl.program_id(0) == 0)
    def _():
        mine = mine_ref[0].astype(jnp.float32)
        for source in range(sources):
            meta = meta_ref[source].astype(jnp.float32)[0:top]
            for column, table in ((2, high_ref), (3, low_ref)):
                value = meta[:, column * tokens : (column + 1) * tokens]
                table[source] = table_at(meta, mine, count, value).astype(jnp.bfloat16)

    for part in range(spread_ref.shape[0]):
        spread_ref[part] = returned_ref[:, part * lanes : (part + 1) * lanes].astype(jnp.float32)
    for source in range(sources):
        rows = jnp.concatenate(
            [
                jnp.concatenate(
                    [
                        spread_ref[
                            part,
                            pl.ds(slot * sources + source, near, stride=CAPACITY * sources),
                            :,
                        ]
                        for part in range(spread_ref.shape[0])
                    ],
                    axis=1,
                )
                for slot in range(CAPACITY)
            ],
            axis=0,
        ).astype(jnp.bfloat16)
        total = sum(
            lax.dot_general(
                table[source], rows, (((0,), (0,)), ((), ())), preferred_element_type=jnp.float32
            )
            for table in (high_ref, low_ref)
        )
        out_ref[source] = total.astype(jnp.bfloat16)


def combine_rows(mine, gathered, returned, tokens, top, columns):
    sources = gathered.shape[0]
    rows, width = returned.shape
    near = rows // CAPACITY // sources
    table = pltpu.VMEM((sources, near * CAPACITY, tokens), jnp.bfloat16)
    return pl.pallas_call(
        functools.partial(combine_kernel, top),
        grid=(width // columns,),
        out_shape=jax.ShapeDtypeStruct((sources, tokens, width), jnp.bfloat16),
        in_specs=[
            pl.BlockSpec(memory_space=pltpu.SMEM),
            pl.BlockSpec((sources, META_ROWS, 4 * tokens), lambda i: (0, tokens // META_ROWS, 0)),
            pl.BlockSpec((rows, columns), lambda i: (0, i)),
        ],
        out_specs=pl.BlockSpec((sources, tokens, columns), lambda i: (0, 0, i)),
        scratch_shapes=[table, table, pltpu.VMEM((columns // LANES, rows, LANES), jnp.float32)],
        compiler_params=pltpu.CompilerParams(vmem_limit_bytes=VMEM_BYTES),
        cost_estimate=pl.CostEstimate(
            flops=4 * rows * tokens * width, bytes_accessed=4 * rows * width, transcendentals=0
        ),
        name="combine_rows",
    )(mine, gathered, returned)


def body(
    queries,
    key_vectors,
    values,
    out_gate,
    write_strength,
    log_fading_factor,
    block_inverse,
    norm_gain,
    hidden,
    routes,
    route_weights,
    gate_weights,
    up_weights,
    down_weights,
):
    tokens, width = hidden.shape
    top = routes.shape[1]
    context_size = lax.axis_size("ctx")
    owner_count = lax.axis_size("exp")
    experts = context_size * owner_count
    chips = context_size // CORES
    side = math.isqrt(owner_count)
    near = chips * side * CORES
    lines, planes = line_groups(chips, side), plane_groups(chips, side)
    core = lax.axis_index("ctx") % CORES
    own_y, own_z = lax.axis_index("exp") // side, lax.axis_index("exp") % side
    mine = jnp.where(core == 0, own_y, own_z).astype(jnp.int32).reshape(1)

    picks = routes.T
    owner = picks % owner_count
    pick_y, pick_z = owner // side, owner % side
    context = picks // owner_count
    pick_x, pick_core = context // CORES, context % CORES
    line = jnp.where(core == 0, pick_y, pick_z).astype(jnp.float32)
    across = jnp.where(core == 0, pick_z, pick_y)
    place = (pick_x * side + across) * CORES + (pick_core + core) % CORES
    place = jnp.stack([place.astype(jnp.float32), jnp.full(place.shape, near, jnp.float32)])

    swap = [(i, i + 1 - 2 * (i % CORES)) for i in range(context_size)]
    own_weights = [gate_weights[0], up_weights[0], down_weights[0]]
    partner_weights = [lax.ppermute(weight, "ctx", swap) for weight in own_weights]

    sent = head_rows(picks, line, place, route_weights.T, hidden, experts, side)
    gathered = exchange(sent, lines).reshape(side, tokens + META_ROWS, width)
    outgoing = pack_rows(mine, gathered, tokens, top, near, width // 4)
    received = exchange(outgoing, planes)
    pieces, incoming_state = delta_front(
        queries, key_vectors, values, write_strength, log_fading_factor, block_inverse
    )
    received, incoming_state = lax.optimization_barrier((received, incoming_state))
    produced = expert_rows(received, own_weights + partner_weights, chips * side, 4)
    returned = exchange(produced, planes)
    partial = combine_rows(mine, gathered, returned, tokens, top, width // 4)
    partial = exchange(partial.reshape(side * tokens, width), lines).reshape(side, tokens, width)
    expert_output = jnp.sum(partial.astype(jnp.float32), axis=0).astype(jnp.bfloat16)
    _, attended = run_blocks(pieces, incoming_state)
    mixer_output = gated_norm(attended.reshape(out_gate.shape), norm_gain, out_gate)
    return (mixer_output, expert_output)


def solution(mesh):
    placed = (
        P("exp", "ctx", None),
        P("exp", "ctx", None),
        P("exp", "ctx", None),
        P("exp", "ctx", None),
        P("exp", "ctx"),
        P("exp", "ctx"),
        P("exp", "ctx", None, None),
        P(),
        P(("ctx", "exp"), None),
        P(("ctx", "exp"), None),
        P(("ctx", "exp"), None),
        P(("ctx", "exp"), None, None),
        P(("ctx", "exp"), None, None),
        P(("ctx", "exp"), None, None),
    )
    return jax.shard_map(
        body,
        mesh=mesh,
        in_specs=placed,
        out_specs=(P("exp", "ctx", None), P(("ctx", "exp"), None)),
        check_vma=False,
    )
```

```python
import functools
import math

import jax
import jax.numpy as jnp
from jax import lax
from jax.experimental import pallas as pl
from jax.experimental.pallas import tpu as pltpu
from jax.sharding import PartitionSpec as P

TOP_PRECISION = lax.Precision.HIGHEST
NORM_EPSILON = 1e-06
CAPACITY = 3
CORES = 2
LANES = 128
META_ROWS = 16
VMEM_BYTES = 40 * 1024 * 1024


def block_parts(queries, key_vectors, values, write_strength, log_fading_factor, block_inverse):
    tracks, length, head_width = queries.shape
    block_size = block_inverse.shape[-1]
    blocks = length // block_size
    shape_four = (tracks, blocks, block_size, head_width)
    query_blocks = queries.reshape(shape_four)
    key_blocks = key_vectors.reshape(shape_four)
    value_blocks = values.reshape(shape_four)
    strength = write_strength.reshape(tracks, blocks, block_size)
    running = jnp.cumsum(log_fading_factor.reshape(tracks, blocks, block_size), axis=-1)
    growth = jnp.exp(running)
    final_log = running[..., -1:]
    write_keys = jnp.einsum(
        "sbij,sbjh->sbih",
        block_inverse,
        key_blocks * (strength * growth)[..., None],
        precision=TOP_PRECISION,
    )
    write_values = jnp.einsum(
        "sbij,sbjh->sbih",
        block_inverse,
        value_blocks * strength[..., None],
        precision=TOP_PRECISION,
    )
    faded_keys = key_blocks * jnp.exp(final_log - running)[..., None]
    faded_queries = query_blocks * growth[..., None]
    row_index = lax.broadcasted_iota(jnp.int32, (block_size, block_size), 0)
    col_index = lax.broadcasted_iota(jnp.int32, (block_size, block_size), 1)
    spread = running[..., :, None] - running[..., None, :]
    causal_fade = jnp.where(row_index >= col_index, jnp.exp(jnp.minimum(spread, 0.0)), 0.0)
    causal = (
        jnp.einsum("sbih,sbjh->sbij", query_blocks, key_blocks, precision=TOP_PRECISION)
        * causal_fade
    )
    return (faded_queries, write_keys, write_values, faded_keys, causal, jnp.exp(final_log))


def block_step(states, pieces):
    faded_queries, write_keys, write_values, faded_keys, causal, decays = pieces
    fresh_values = write_values - jnp.einsum(
        "sch,shv->scv", write_keys, states, precision=TOP_PRECISION
    )
    attended = jnp.einsum("sch,shv->scv", faded_queries, states, precision=TOP_PRECISION)
    attended = attended + jnp.einsum("sij,sjv->siv", causal, fresh_values, precision=TOP_PRECISION)
    states = decays[..., None] * states + jnp.einsum(
        "sch,scv->shv", faded_keys, fresh_values, precision=TOP_PRECISION
    )
    return (states, attended)


def run_blocks(pieces, states):
    moved = tuple((jnp.moveaxis(piece_item, 1, 0) for piece_item in pieces))
    states, attended = lax.scan(block_step, states, moved)
    return (states, jnp.moveaxis(attended, 0, 1))


def gated_norm(attended, norm_gain, out_gate):
    root_mean = jnp.sqrt(jnp.mean(attended * attended, axis=-1, keepdims=True) + NORM_EPSILON)
    return attended / root_mean * norm_gain * jax.nn.silu(out_gate)


def compose(carried, block_piece):
    current_mapping, current_addend = carried
    segment_mapping, segment_addend = block_piece
    updated_mapping = jnp.einsum(
        "qfz,qze->qfe", segment_mapping, current_mapping, precision=TOP_PRECISION
    )
    updated_addend = (
        jnp.einsum("qfz,qze->qfe", segment_mapping, current_addend, precision=TOP_PRECISION)
        + segment_addend
    )
    return ((updated_mapping, updated_addend), None)


def delta_front(queries, key_vectors, values, write_strength, log_fading_factor, block_inverse):
    tracks, length, head_width = queries.shape
    pieces = block_parts(
        queries, key_vectors, values, write_strength, log_fading_factor, block_inverse
    )
    faded_queries, write_keys, write_values, faded_keys, causal, decays = pieces
    unit_matrix = jnp.eye(head_width, dtype=jnp.float32)
    identity_map = jnp.broadcast_to(unit_matrix, (tracks, head_width, head_width))
    block_maps = decays[..., None] * unit_matrix - jnp.einsum(
        "sbch,sbck->sbhk", faded_keys, write_keys, precision=TOP_PRECISION
    )
    block_adds = jnp.einsum("sbch,sbcv->sbhv", faded_keys, write_values, precision=TOP_PRECISION)
    (section_mapping, section_addend), _ = lax.scan(
        compose,
        (identity_map, jnp.zeros_like(identity_map)),
        (jnp.moveaxis(block_maps, 1, 0), jnp.moveaxis(block_adds, 1, 0)),
    )
    return pieces, jnp.concatenate([section_mapping, section_addend], axis=0)


def entering_state(sections):
    maps, addends = sections[:, 0], sections[:, 1]
    mine = lax.axis_index("ctx")
    state = addends[0]
    for section in range(1, sections.shape[0] - 1):
        later = jnp.dot(maps[section], state, precision=TOP_PRECISION) + addends[section]
        state = jnp.where(section < mine, later, state)
    return jnp.where(mine == 0, 0.0, state)[None]


def device_of(x, core, y, z, side):
    return ((x * CORES + core) * side + y) * side + z


def line_groups(chips, side):
    first = [[device_of(x, 0, y, z, side) for y in range(side)] for x in range(chips) for z in range(side)]
    second = [[device_of(x, 1, y, z, side) for z in range(side)] for x in range(chips) for y in range(side)]
    return first + second


def plane_groups(chips, side):
    first = [[device_of(x, 0, y, z, side) for x in range(chips) for z in range(side)] for y in range(side)]
    second = [[device_of(x, 1, y, z, side) for x in range(chips) for y in range(side)] for z in range(side)]
    return first + second


def exchange(rows, groups):
    return lax.all_to_all(
        rows, ("ctx", "exp"), split_axis=0, concat_axis=0, tiled=True, axis_index_groups=groups
    )


def head_kernel(experts, picks_ref, line_ref, place_ref, weights_ref, out_ref, block_ref):
    top, tokens = picks_ref.shape
    picks = picks_ref[...]
    row = lax.broadcasted_iota(jnp.int32, (experts, tokens), 0)
    named = jnp.zeros((experts, tokens), jnp.bool_)
    for pick in range(top):
        named = jnp.logical_or(named, picks[pick : pick + 1, :] == row)
    before = lax.broadcasted_iota(jnp.int32, (tokens, tokens), 0) < lax.broadcasted_iota(
        jnp.int32, (tokens, tokens), 1
    )
    earlier = jnp.dot(
        named.astype(jnp.float32).astype(jnp.bfloat16),
        before.astype(jnp.float32).astype(jnp.bfloat16),
        preferred_element_type=jnp.float32,
    )
    slot = jnp.concatenate(
        [
            jnp.sum(jnp.where(picks[pick : pick + 1, :] == row, earlier, 0.0), axis=0, keepdims=True)
            for pick in range(top)
        ],
        axis=0,
    )
    weights = weights_ref[...]
    high = weights.astype(jnp.bfloat16).astype(jnp.float32)
    block_ref[...] = jnp.zeros_like(block_ref)
    for column, item in enumerate(
        (line_ref[...], place_ref[0] + slot * place_ref[1], high, weights - high)
    ):
        block_ref[0:top, column * tokens : (column + 1) * tokens] = item
    out_ref[...] = block_ref[...].astype(jnp.bfloat16)


def head_rows(picks, line, place, weights, experts):
    shape = (META_ROWS, 4 * picks.shape[1])
    return pl.pallas_call(
        functools.partial(head_kernel, experts),
        out_shape=jax.ShapeDtypeStruct(shape, jnp.bfloat16),
        scratch_shapes=[pltpu.VMEM(shape, jnp.float32)],
        compiler_params=pltpu.CompilerParams(vmem_limit_bytes=16 * 1024 * 1024),
        cost_estimate=pl.CostEstimate(
            flops=60 * experts * picks.shape[1], bytes_accessed=65536, transcendentals=0
        ),
        name="head_rows",
    )(picks, line, place, weights)


def table_at(meta, mine, count, value):
    tokens = value.shape[1]
    row = lax.broadcasted_iota(jnp.int32, (count, tokens), 0).astype(jnp.float32)
    place = jnp.where(meta[:, 0:tokens] == mine, meta[:, tokens : 2 * tokens], -1.0)
    table = jnp.zeros((count, tokens), jnp.float32)
    for pick in range(value.shape[0]):
        table = jnp.where(place[pick : pick + 1, :] == row, value[pick : pick + 1, :], table)
    return table


def pack_kernel(top, mine_ref, meta_ref, data_ref, out_ref, table_ref, spread_ref):
    sources, tokens, _ = data_ref.shape
    count = table_ref.shape[1]
    near = count // CAPACITY
    lanes = spread_ref.shape[2]

    @pl.when(pl.program_id(0) == 0)
    def _():
        mine = mine_ref[0].astype(jnp.float32)
        for source in range(sources):
            meta = meta_ref[source].astype(jnp.float32)[0:top]
            ones = jnp.ones((top, tokens), jnp.float32)
            table_ref[source] = table_at(meta, mine, count, ones).astype(jnp.bfloat16)

    for source in range(sources):
        rows = jnp.dot(table_ref[source], data_ref[source], preferred_element_type=jnp.float32)
        for slot in range(CAPACITY):
            at = pl.ds(slot * sources + source, near, stride=CAPACITY * sources)
            for part in range(spread_ref.shape[0]):
                spread_ref[part, at, :] = rows[
                    slot * near : (slot + 1) * near, part * lanes : (part + 1) * lanes
                ]
    for part in range(spread_ref.shape[0]):
        out_ref[:, part * lanes : (part + 1) * lanes] = spread_ref[part].astype(jnp.bfloat16)


def pack_rows(mine, meta, data, top, near, columns):
    sources, tokens, width = data.shape
    rows = near * CAPACITY * sources
    return pl.pallas_call(
        functools.partial(pack_kernel, top),
        grid=(width // columns,),
        out_shape=pltpu.HBM((rows, width), jnp.bfloat16),
        in_specs=[
            pl.BlockSpec(memory_space=pltpu.SMEM),
            pl.BlockSpec(meta.shape, lambda i: (0, 0, 0)),
            pl.BlockSpec((sources, tokens, columns), lambda i: (0, 0, i)),
        ],
        out_specs=pl.BlockSpec((rows, columns), lambda i: (0, i)),
        scratch_shapes=[
            pltpu.VMEM((sources, near * CAPACITY, tokens), jnp.bfloat16),
            pltpu.VMEM((columns // LANES, rows, LANES), jnp.float32),
        ],
        compiler_params=pltpu.CompilerParams(vmem_limit_bytes=VMEM_BYTES),
        cost_estimate=pl.CostEstimate(
            flops=2 * rows * tokens * width, bytes_accessed=4 * rows * width, transcendentals=0
        ),
        name="pack_rows",
    )(mine, meta, data)


def expert_kernel(received_ref, *refs):
    weight_refs, out_ref, here = refs[:6], refs[6], refs[7:13]
    spread_ref, ready = refs[13:]
    loads = [
        pltpu.make_async_copy(there, place, ready.at[i])
        for i, (there, place) in enumerate(zip(weight_refs, here))
    ]
    first = pl.program_id(0) == 0

    @pl.when(first)
    def _():
        for load in loads:
            load.start()

    senders, each, width = spread_ref.shape
    half = each // CORES
    spread_ref[...] = received_ref[...].astype(jnp.float32).reshape(spread_ref.shape)
    for turn in range(CORES):
        at = pl.ds(turn * half, half)
        rows = spread_ref[:, at, :].reshape(senders * half, width).astype(jnp.bfloat16)

        @pl.when(first)
        def _():
            for load in loads[3 * turn : 3 * turn + 3]:
                load.wait()

        gate_here, up_here, down_here = here[3 * turn : 3 * turn + 3]
        gate = jnp.dot(rows, gate_here[...], preferred_element_type=jnp.float32)
        up = jnp.dot(rows, up_here[...], preferred_element_type=jnp.float32)
        active = (gate / (1.0 + jnp.exp(-gate)) * up).astype(jnp.bfloat16)
        produced = jnp.dot(active, down_here[...], preferred_element_type=jnp.float32)
        spread_ref[:, at, :] = produced.reshape(senders, half, width)
    out_ref[...] = spread_ref[...].reshape(out_ref.shape).astype(jnp.bfloat16)


def expert_rows(received, weights, senders, steps):
    rows, width = received.shape
    units = weights[0].shape[1]
    block = pl.BlockSpec((rows // steps, width), lambda i: (i, 0))
    whole = pl.BlockSpec(memory_space=pl.ANY)
    return pl.pallas_call(
        expert_kernel,
        grid=(steps,),
        out_shape=pltpu.HBM(received.shape, jnp.bfloat16),
        in_specs=[block] + [whole] * len(weights),
        out_specs=block,
        scratch_shapes=[pltpu.VMEM(weight.shape, jnp.bfloat16) for weight in weights]
        + [
            pltpu.VMEM((senders // steps, rows // senders, width), jnp.float32),
            pltpu.SemaphoreType.DMA((len(weights),)),
        ],
        compiler_params=pltpu.CompilerParams(vmem_limit_bytes=VMEM_BYTES),
        cost_estimate=pl.CostEstimate(
            flops=6 * rows * width * units,
            bytes_accessed=4 * rows * width + 12 * width * units,
            transcendentals=rows * units,
        ),
        name="expert_rows",
    )(received, *weights)


def combine_kernel(top, mine_ref, meta_ref, returned_ref, out_ref, high_ref, low_ref, spread_ref):
    sources, tokens, _ = out_ref.shape
    count = high_ref.shape[1]
    near = count // CAPACITY
    lanes = spread_ref.shape[2]

    @pl.when(pl.program_id(0) == 0)
    def _():
        mine = mine_ref[0].astype(jnp.float32)
        for source in range(sources):
            meta = meta_ref[source].astype(jnp.float32)[0:top]
            for column, table in ((2, high_ref), (3, low_ref)):
                value = meta[:, column * tokens : (column + 1) * tokens]
                table[source] = table_at(meta, mine, count, value).astype(jnp.bfloat16)

    for part in range(spread_ref.shape[0]):
        spread_ref[part] = returned_ref[:, part * lanes : (part + 1) * lanes].astype(jnp.float32)
    for source in range(sources):
        rows = jnp.concatenate(
            [
                jnp.concatenate(
                    [
                        spread_ref[
                            part,
                            pl.ds(slot * sources + source, near, stride=CAPACITY * sources),
                            :,
                        ]
                        for part in range(spread_ref.shape[0])
                    ],
                    axis=1,
                )
                for slot in range(CAPACITY)
            ],
            axis=0,
        ).astype(jnp.bfloat16)
        total = sum(
            lax.dot_general(
                table[source], rows, (((0,), (0,)), ((), ())), preferred_element_type=jnp.float32
            )
            for table in (high_ref, low_ref)
        )
        out_ref[source] = total.astype(jnp.bfloat16)


def combine_rows(mine, meta, returned, tokens, top, columns):
    sources = meta.shape[0]
    rows, width = returned.shape
    near = rows // CAPACITY // sources
    table = pltpu.VMEM((sources, near * CAPACITY, tokens), jnp.bfloat16)
    return pl.pallas_call(
        functools.partial(combine_kernel, top),
        grid=(width // columns,),
        out_shape=pltpu.HBM((sources, tokens, width), jnp.bfloat16),
        in_specs=[
            pl.BlockSpec(memory_space=pltpu.SMEM),
            pl.BlockSpec(meta.shape, lambda i: (0, 0, 0)),
            pl.BlockSpec((rows, columns), lambda i: (0, i)),
        ],
        out_specs=pl.BlockSpec((sources, tokens, columns), lambda i: (0, 0, i)),
        scratch_shapes=[table, table, pltpu.VMEM((columns // LANES, rows, LANES), jnp.float32)],
        compiler_params=pltpu.CompilerParams(vmem_limit_bytes=VMEM_BYTES),
        cost_estimate=pl.CostEstimate(
            flops=4 * rows * tokens * width, bytes_accessed=4 * rows * width, transcendentals=0
        ),
        name="combine_rows",
    )(mine, meta, returned)


def body(
    queries,
    key_vectors,
    values,
    out_gate,
    write_strength,
    log_fading_factor,
    block_inverse,
    norm_gain,
    hidden,
    routes,
    route_weights,
    gate_weights,
    up_weights,
    down_weights,
):
    tokens, width = hidden.shape
    top = routes.shape[1]
    context_size = lax.axis_size("ctx")
    owner_count = lax.axis_size("exp")
    experts = context_size * owner_count
    chips = context_size // CORES
    side = math.isqrt(owner_count)
    near = chips * side * CORES
    lines, planes = line_groups(chips, side), plane_groups(chips, side)
    core = lax.axis_index("ctx") % CORES
    own_y, own_z = lax.axis_index("exp") // side, lax.axis_index("exp") % side
    mine = jnp.where(core == 0, own_y, own_z).astype(jnp.int32).reshape(1)

    picks = routes.T
    owner = picks % owner_count
    pick_y, pick_z = owner // side, owner % side
    context = picks // owner_count
    pick_x, pick_core = context // CORES, context % CORES
    line = jnp.where(core == 0, pick_y, pick_z).astype(jnp.float32)
    across = jnp.where(core == 0, pick_z, pick_y)
    place = (pick_x * side + across) * CORES + (pick_core + core) % CORES
    place = jnp.stack([place.astype(jnp.float32), jnp.full(place.shape, near, jnp.float32)])

    copies = jnp.broadcast_to(hidden[None], (side, tokens, width)).reshape(side * tokens, width)
    copies, picks = lax.optimization_barrier((copies, picks))
    data = exchange(copies, lines).reshape(side, tokens, width)
    meta = lax.all_gather(
        head_rows(picks, line, place, route_weights.T, experts),
        ("ctx", "exp"),
        axis_index_groups=lines,
    )
    swap = [(i, i + 1 - 2 * (i % CORES)) for i in range(context_size)]
    own_weights = [gate_weights[0], up_weights[0], down_weights[0]]
    partner_weights = [lax.ppermute(weight, "ctx", swap) for weight in own_weights]
    pieces, section = delta_front(
        queries, key_vectors, values, write_strength, log_fading_factor, block_inverse
    )
    data, partner_weights = lax.optimization_barrier((data, partner_weights))
    outgoing = pack_rows(mine, meta, data, top, near, width // 4)
    outgoing, section = lax.optimization_barrier((outgoing, section))
    received = exchange(outgoing, planes)
    sections = lax.all_gather(section, "ctx")
    produced = expert_rows(received, own_weights + partner_weights, chips * side, 4)
    returned = exchange(produced, planes)
    partial = combine_rows(mine, meta, returned, tokens, top, width // 4)
    partial = exchange(partial.reshape(side * tokens, width), lines).reshape(side, tokens, width)
    expert_output = jnp.sum(partial.astype(jnp.float32), axis=0).astype(jnp.bfloat16)
    _, attended = run_blocks(pieces, entering_state(sections))
    mixer_output = gated_norm(attended.reshape(out_gate.shape), norm_gain, out_gate)
    return (mixer_output, expert_output)


def solution(mesh):
    placed = (
        P("exp", "ctx", None),
        P("exp", "ctx", None),
        P("exp", "ctx", None),
        P("exp", "ctx", None),
        P("exp", "ctx"),
        P("exp", "ctx"),
        P("exp", "ctx", None, None),
        P(),
        P(("ctx", "exp"), None),
        P(("ctx", "exp"), None),
        P(("ctx", "exp"), None),
        P(("ctx", "exp"), None, None),
        P(("ctx", "exp"), None, None),
        P(("ctx", "exp"), None, None),
    )
    return jax.shard_map(
        body,
        mesh=mesh,
        in_specs=placed,
        out_specs=(P("exp", "ctx", None), P(("ctx", "exp"), None)),
        check_vma=False,
    )
```

```python
import functools
import math

import jax
import jax.numpy as jnp
from jax import lax
from jax.experimental import pallas as pl
from jax.experimental.pallas import tpu as pltpu
from jax.sharding import PartitionSpec as P

TOP_PRECISION = lax.Precision.HIGHEST
NORM_EPSILON = 1e-06
CAPACITY = 3
CORES = 2
LANES = 128
META_ROWS = 16
VMEM_BYTES = 40 * 1024 * 1024


def block_parts(queries, key_vectors, values, write_strength, log_fading_factor, block_inverse):
    tracks, length, head_width = queries.shape
    block_size = block_inverse.shape[-1]
    blocks = length // block_size
    shape_four = (tracks, blocks, block_size, head_width)
    query_blocks = queries.reshape(shape_four)
    key_blocks = key_vectors.reshape(shape_four)
    value_blocks = values.reshape(shape_four)
    strength = write_strength.reshape(tracks, blocks, block_size)
    running = jnp.cumsum(log_fading_factor.reshape(tracks, blocks, block_size), axis=-1)
    growth = jnp.exp(running)
    final_log = running[..., -1:]
    write_keys = jnp.einsum(
        "sbij,sbjh->sbih",
        block_inverse,
        key_blocks * (strength * growth)[..., None],
        precision=TOP_PRECISION,
    )
    write_values = jnp.einsum(
        "sbij,sbjh->sbih",
        block_inverse,
        value_blocks * strength[..., None],
        precision=TOP_PRECISION,
    )
    faded_keys = key_blocks * jnp.exp(final_log - running)[..., None]
    faded_queries = query_blocks * growth[..., None]
    row_index = lax.broadcasted_iota(jnp.int32, (block_size, block_size), 0)
    col_index = lax.broadcasted_iota(jnp.int32, (block_size, block_size), 1)
    spread = running[..., :, None] - running[..., None, :]
    causal_fade = jnp.where(row_index >= col_index, jnp.exp(jnp.minimum(spread, 0.0)), 0.0)
    causal = (
        jnp.einsum("sbih,sbjh->sbij", query_blocks, key_blocks, precision=TOP_PRECISION)
        * causal_fade
    )
    return (faded_queries, write_keys, write_values, faded_keys, causal, jnp.exp(final_log))


def block_step(states, pieces):
    faded_queries, write_keys, write_values, faded_keys, causal, decays = pieces
    fresh_values = write_values - jnp.einsum(
        "sch,shv->scv", write_keys, states, precision=TOP_PRECISION
    )
    attended = jnp.einsum("sch,shv->scv", faded_queries, states, precision=TOP_PRECISION)
    attended = attended + jnp.einsum("sij,sjv->siv", causal, fresh_values, precision=TOP_PRECISION)
    states = decays[..., None] * states + jnp.einsum(
        "sch,scv->shv", faded_keys, fresh_values, precision=TOP_PRECISION
    )
    return (states, attended)


def run_blocks(pieces, states):
    moved = tuple((jnp.moveaxis(piece_item, 1, 0) for piece_item in pieces))
    states, attended = lax.scan(block_step, states, moved)
    return (states, jnp.moveaxis(attended, 0, 1))


def gated_norm(attended, norm_gain, out_gate):
    root_mean = jnp.sqrt(jnp.mean(attended * attended, axis=-1, keepdims=True) + NORM_EPSILON)
    return attended / root_mean * norm_gain * jax.nn.silu(out_gate)


def compose(carried, block_piece):
    current_mapping, current_addend = carried
    segment_mapping, segment_addend = block_piece
    updated_mapping = jnp.einsum(
        "qfz,qze->qfe", segment_mapping, current_mapping, precision=TOP_PRECISION
    )
    updated_addend = (
        jnp.einsum("qfz,qze->qfe", segment_mapping, current_addend, precision=TOP_PRECISION)
        + segment_addend
    )
    return ((updated_mapping, updated_addend), None)


def delta_front(queries, key_vectors, values, write_strength, log_fading_factor, block_inverse):
    tracks, length, head_width = queries.shape
    pieces = block_parts(
        queries, key_vectors, values, write_strength, log_fading_factor, block_inverse
    )
    faded_queries, write_keys, write_values, faded_keys, causal, decays = pieces
    unit_matrix = jnp.eye(head_width, dtype=jnp.float32)
    identity_map = jnp.broadcast_to(unit_matrix, (tracks, head_width, head_width))
    block_maps = decays[..., None] * unit_matrix - jnp.einsum(
        "sbch,sbck->sbhk", faded_keys, write_keys, precision=TOP_PRECISION
    )
    block_adds = jnp.einsum("sbch,sbcv->sbhv", faded_keys, write_values, precision=TOP_PRECISION)
    (section_mapping, section_addend), _ = lax.scan(
        compose,
        (identity_map, jnp.zeros_like(identity_map)),
        (jnp.moveaxis(block_maps, 1, 0), jnp.moveaxis(block_adds, 1, 0)),
    )
    return pieces, jnp.concatenate([section_mapping, section_addend], axis=0)


def earlier_sections(section):
    size = lax.axis_size("ctx")
    return tuple(
        lax.ppermute(section, "ctx", [(i, i + back) for i in range(size - back)])
        for back in range(size - 1, 0, -1)
    )


def entering_state(sections):
    state = sections[0][1:2]
    for section in sections[1:]:
        state = (
            jnp.einsum("qfz,qze->qfe", section[0:1], state, precision=TOP_PRECISION) + section[1:2]
        )
    return state


def device_of(x, core, y, z, side):
    return ((x * CORES + core) * side + y) * side + z


def line_groups(chips, side):
    first = [[device_of(x, 0, y, z, side) for y in range(side)] for x in range(chips) for z in range(side)]
    second = [[device_of(x, 1, y, z, side) for z in range(side)] for x in range(chips) for y in range(side)]
    return first + second


def plane_groups(chips, side):
    first = [[device_of(x, 0, y, z, side) for x in range(chips) for z in range(side)] for y in range(side)]
    second = [[device_of(x, 1, y, z, side) for x in range(chips) for y in range(side)] for z in range(side)]
    return first + second


def exchange(rows, groups):
    return lax.all_to_all(
        rows, ("ctx", "exp"), split_axis=0, concat_axis=0, tiled=True, axis_index_groups=groups
    )


def head_kernel(
    experts, copies, picks_ref, line_ref, place_ref, weights_ref, hidden_ref, out_ref, block_ref, meta_ref, sent
):
    top, tokens = picks_ref.shape
    each = out_ref.shape[0] // copies
    moves = [
        pltpu.make_async_copy(hidden_ref, out_ref.at[pl.ds(copy * each, tokens), :], sent.at[copy])
        for copy in range(copies)
    ]
    for move in moves:
        move.start()
    picks = picks_ref[...]
    row = lax.broadcasted_iota(jnp.int32, (experts, tokens), 0)
    named = jnp.zeros((experts, tokens), jnp.bool_)
    for pick in range(top):
        named = jnp.logical_or(named, picks[pick : pick + 1, :] == row)
    before = lax.broadcasted_iota(jnp.int32, (tokens, tokens), 0) < lax.broadcasted_iota(
        jnp.int32, (tokens, tokens), 1
    )
    earlier = jnp.dot(
        named.astype(jnp.float32).astype(jnp.bfloat16),
        before.astype(jnp.float32).astype(jnp.bfloat16),
        preferred_element_type=jnp.float32,
    )
    slot = jnp.concatenate(
        [
            jnp.sum(jnp.where(picks[pick : pick + 1, :] == row, earlier, 0.0), axis=0, keepdims=True)
            for pick in range(top)
        ],
        axis=0,
    )
    weights = weights_ref[...]
    high = weights.astype(jnp.bfloat16).astype(jnp.float32)
    block_ref[...] = jnp.zeros_like(block_ref)
    for column, item in enumerate(
        (line_ref[...], place_ref[0] + slot * place_ref[1], high, weights - high)
    ):
        block_ref[0:top, column * tokens : (column + 1) * tokens] = item
    meta_ref[...] = block_ref[...].astype(jnp.bfloat16)
    more = [
        pltpu.make_async_copy(
            meta_ref, out_ref.at[pl.ds(copy * each + tokens, META_ROWS), :], sent.at[copies + copy]
        )
        for copy in range(copies)
    ]
    for move in more:
        move.start()
    for move in moves + more:
        move.wait()


def head_rows(picks, line, place, weights, hidden, experts, copies):
    tokens, width = hidden.shape
    here = pl.BlockSpec(memory_space=pltpu.VMEM)
    return pl.pallas_call(
        functools.partial(head_kernel, experts, copies),
        out_shape=pltpu.HBM((copies * (tokens + META_ROWS), width), jnp.bfloat16),
        in_specs=[here] * 5,
        out_specs=pl.BlockSpec(memory_space=pl.ANY),
        scratch_shapes=[
            pltpu.VMEM((META_ROWS, width), jnp.float32),
            pltpu.VMEM((META_ROWS, width), jnp.bfloat16),
            pltpu.SemaphoreType.DMA((2 * copies,)),
        ],
        compiler_params=pltpu.CompilerParams(vmem_limit_bytes=16 * 1024 * 1024),
        cost_estimate=pl.CostEstimate(
            flops=60 * experts * tokens, bytes_accessed=2 * copies * tokens * width, transcendentals=0
        ),
        name="head_rows",
    )(picks, line, place, weights, hidden)


def table_at(meta, mine, count, value):
    tokens = value.shape[1]
    row = lax.broadcasted_iota(jnp.int32, (count, tokens), 0).astype(jnp.float32)
    place = jnp.where(meta[:, 0:tokens] == mine, meta[:, tokens : 2 * tokens], -1.0)
    table = jnp.zeros((count, tokens), jnp.float32)
    for pick in range(value.shape[0]):
        table = jnp.where(place[pick : pick + 1, :] == row, value[pick : pick + 1, :], table)
    return table


def pack_kernel(top, mine_ref, meta_ref, data_ref, out_ref, table_ref, spread_ref):
    sources, tokens, _ = data_ref.shape
    count = table_ref.shape[1]
    near = count // CAPACITY
    lanes = spread_ref.shape[2]

    @pl.when(pl.program_id(0) == 0)
    def _():
        mine = mine_ref[0].astype(jnp.float32)
        for source in range(sources):
            meta = meta_ref[source].astype(jnp.float32)[0:top]
            ones = jnp.ones((top, tokens), jnp.float32)
            table_ref[source] = table_at(meta, mine, count, ones).astype(jnp.bfloat16)

    for source in range(sources):
        rows = jnp.dot(table_ref[source], data_ref[source], preferred_element_type=jnp.float32)
        for slot in range(CAPACITY):
            at = pl.ds(slot * sources + source, near, stride=CAPACITY * sources)
            for part in range(spread_ref.shape[0]):
                spread_ref[part, at, :] = rows[
                    slot * near : (slot + 1) * near, part * lanes : (part + 1) * lanes
                ]
    for part in range(spread_ref.shape[0]):
        out_ref[:, part * lanes : (part + 1) * lanes] = spread_ref[part].astype(jnp.bfloat16)


def pack_rows(mine, gathered, tokens, top, near, columns):
    sources, _, width = gathered.shape
    rows = near * CAPACITY * sources
    return pl.pallas_call(
        functools.partial(pack_kernel, top),
        grid=(width // columns,),
        out_shape=pltpu.HBM((rows, width), jnp.bfloat16),
        in_specs=[
            pl.BlockSpec(memory_space=pltpu.SMEM),
            pl.BlockSpec((sources, META_ROWS, 4 * tokens), lambda i: (0, tokens // META_ROWS, 0)),
            pl.BlockSpec((sources, tokens, columns), lambda i: (0, 0, i)),
        ],
        out_specs=pl.BlockSpec((rows, columns), lambda i: (0, i)),
        scratch_shapes=[
            pltpu.VMEM((sources, near * CAPACITY, tokens), jnp.bfloat16),
            pltpu.VMEM((columns // LANES, rows, LANES), jnp.float32),
        ],
        compiler_params=pltpu.CompilerParams(vmem_limit_bytes=VMEM_BYTES),
        cost_estimate=pl.CostEstimate(
            flops=2 * rows * tokens * width, bytes_accessed=4 * rows * width, transcendentals=0
        ),
        name="pack_rows",
    )(mine, gathered, gathered)


def expert_kernel(received_ref, *refs):
    weight_refs, out_ref, here = refs[:6], refs[6], refs[7:13]
    spread_ref, ready = refs[13:]
    loads = [
        pltpu.make_async_copy(there, place, ready.at[i])
        for i, (there, place) in enumerate(zip(weight_refs, here))
    ]
    first = pl.program_id(0) == 0

    @pl.when(first)
    def _():
        for load in loads:
            load.start()

    senders, each, width = spread_ref.shape
    half = each // CORES
    spread_ref[...] = received_ref[...].astype(jnp.float32).reshape(spread_ref.shape)
    for turn in range(CORES):
        at = pl.ds(turn * half, half)
        rows = spread_ref[:, at, :].reshape(senders * half, width).astype(jnp.bfloat16)

        @pl.when(first)
        def _():
            for load in loads[3 * turn : 3 * turn + 3]:
                load.wait()

        gate_here, up_here, down_here = here[3 * turn : 3 * turn + 3]
        gate = jnp.dot(rows, gate_here[...], preferred_element_type=jnp.float32)
        up = jnp.dot(rows, up_here[...], preferred_element_type=jnp.float32)
        active = (gate / (1.0 + jnp.exp(-gate)) * up).astype(jnp.bfloat16)
        produced = jnp.dot(active, down_here[...], preferred_element_type=jnp.float32)
        spread_ref[:, at, :] = produced.reshape(senders, half, width)
    out_ref[...] = spread_ref[...].reshape(out_ref.shape).astype(jnp.bfloat16)


def expert_rows(received, weights, senders, steps):
    rows, width = received.shape
    units = weights[0].shape[1]
    block = pl.BlockSpec((rows // steps, width), lambda i: (i, 0))
    whole = pl.BlockSpec(memory_space=pl.ANY)
    return pl.pallas_call(
        expert_kernel,
        grid=(steps,),
        out_shape=pltpu.HBM(received.shape, jnp.bfloat16),
        in_specs=[block] + [whole] * len(weights),
        out_specs=block,
        scratch_shapes=[pltpu.VMEM(weight.shape, jnp.bfloat16) for weight in weights]
        + [
            pltpu.VMEM((senders // steps, rows // senders, width), jnp.float32),
            pltpu.SemaphoreType.DMA((len(weights),)),
        ],
        compiler_params=pltpu.CompilerParams(vmem_limit_bytes=VMEM_BYTES),
        cost_estimate=pl.CostEstimate(
            flops=6 * rows * width * units,
            bytes_accessed=4 * rows * width + 12 * width * units,
            transcendentals=rows * units,
        ),
        name="expert_rows",
    )(received, *weights)


def combine_kernel(top, mine_ref, meta_ref, returned_ref, out_ref, table_ref, spread_ref):
    sources, tokens, _ = out_ref.shape
    count = table_ref.shape[1]
    near = count // CAPACITY
    lanes = spread_ref.shape[2]

    @pl.when(pl.program_id(0) == 0)
    def _():
        mine = mine_ref[0].astype(jnp.float32)
        for source in range(sources):
            meta = meta_ref[source].astype(jnp.float32)[0:top]
            for half in range(2):
                value = meta[:, (2 + half) * tokens : (3 + half) * tokens]
                table_ref[source, :, half * tokens : (half + 1) * tokens] = table_at(
                    meta, mine, count, value
                ).astype(jnp.bfloat16)

    for part in range(spread_ref.shape[0]):
        spread_ref[part] = returned_ref[:, part * lanes : (part + 1) * lanes].astype(jnp.float32)
    for source in range(sources):
        rows = jnp.concatenate(
            [
                jnp.concatenate(
                    [
                        spread_ref[
                            part,
                            pl.ds(slot * sources + source, near, stride=CAPACITY * sources),
                            :,
                        ]
                        for part in range(spread_ref.shape[0])
                    ],
                    axis=1,
                )
                for slot in range(CAPACITY)
            ],
            axis=0,
        ).astype(jnp.bfloat16)
        total = lax.dot_general(
            table_ref[source], rows, (((0,), (0,)), ((), ())), preferred_element_type=jnp.float32
        )
        out_ref[source] = (total[:tokens] + total[tokens:]).astype(jnp.bfloat16)


def combine_rows(mine, gathered, returned, tokens, top, columns):
    sources = gathered.shape[0]
    rows, width = returned.shape
    near = rows // CAPACITY // sources
    return pl.pallas_call(
        functools.partial(combine_kernel, top),
        grid=(width // columns,),
        out_shape=pltpu.HBM((sources, tokens, width), jnp.bfloat16),
        in_specs=[
            pl.BlockSpec(memory_space=pltpu.SMEM),
            pl.BlockSpec((sources, META_ROWS, 4 * tokens), lambda i: (0, tokens // META_ROWS, 0)),
            pl.BlockSpec((rows, columns), lambda i: (0, i)),
        ],
        out_specs=pl.BlockSpec((sources, tokens, columns), lambda i: (0, 0, i)),
        scratch_shapes=[
            pltpu.VMEM((sources, near * CAPACITY, 2 * tokens), jnp.bfloat16),
            pltpu.VMEM((columns // LANES, rows, LANES), jnp.float32),
        ],
        compiler_params=pltpu.CompilerParams(vmem_limit_bytes=VMEM_BYTES),
        cost_estimate=pl.CostEstimate(
            flops=4 * rows * tokens * width, bytes_accessed=4 * rows * width, transcendentals=0
        ),
        name="combine_rows",
    )(mine, gathered, returned)


def body(
    queries,
    key_vectors,
    values,
    out_gate,
    write_strength,
    log_fading_factor,
    block_inverse,
    norm_gain,
    hidden,
    routes,
    route_weights,
    gate_weights,
    up_weights,
    down_weights,
):
    tokens, width = hidden.shape
    top = routes.shape[1]
    context_size = lax.axis_size("ctx")
    owner_count = lax.axis_size("exp")
    experts = context_size * owner_count
    chips = context_size // CORES
    side = math.isqrt(owner_count)
    near = chips * side * CORES
    lines, planes = line_groups(chips, side), plane_groups(chips, side)
    core = lax.axis_index("ctx") % CORES
    own_y, own_z = lax.axis_index("exp") // side, lax.axis_index("exp") % side
    mine = jnp.where(core == 0, own_y, own_z).astype(jnp.int32).reshape(1)

    picks = routes.T
    owner = picks % owner_count
    pick_y, pick_z = owner // side, owner % side
    context = picks // owner_count
    pick_x, pick_core = context // CORES, context % CORES
    line = jnp.where(core == 0, pick_y, pick_z).astype(jnp.float32)
    across = jnp.where(core == 0, pick_z, pick_y)
    place = (pick_x * side + across) * CORES + (pick_core + core) % CORES
    place = jnp.stack([place.astype(jnp.float32), jnp.full(place.shape, near, jnp.float32)])

    sent = head_rows(picks, line, place, route_weights.T, hidden, experts, side)
    gathered = exchange(sent, lines).reshape(side, tokens + META_ROWS, width)
    swap = [(i, i + 1 - 2 * (i % CORES)) for i in range(context_size)]
    own_weights = [gate_weights[0], up_weights[0], down_weights[0]]
    partner_weights = [lax.ppermute(weight, "ctx", swap) for weight in own_weights]
    pieces, section = delta_front(
        queries, key_vectors, values, write_strength, log_fading_factor, block_inverse
    )
    gathered, partner_weights, section = lax.optimization_barrier(
        (gathered, partner_weights, section)
    )
    outgoing = pack_rows(mine, gathered, tokens, top, near, width // 4)
    received = exchange(outgoing, planes)
    received, sections = lax.optimization_barrier((received, earlier_sections(section)))
    produced = expert_rows(received, own_weights + partner_weights, chips * side, 2)
    returned = exchange(produced, planes)
    partial = combine_rows(mine, gathered, returned, tokens, top, width // 4)
    partial = exchange(partial.reshape(side * tokens, width), lines).reshape(side, tokens, width)
    expert_output = jnp.sum(partial.astype(jnp.float32), axis=0).astype(jnp.bfloat16)
    _, attended = run_blocks(pieces, entering_state(sections))
    mixer_output = gated_norm(attended.reshape(out_gate.shape), norm_gain, out_gate)
    return (mixer_output, expert_output)


def solution(mesh):
    placed = (
        P("exp", "ctx", None),
        P("exp", "ctx", None),
        P("exp", "ctx", None),
        P("exp", "ctx", None),
        P("exp", "ctx"),
        P("exp", "ctx"),
        P("exp", "ctx", None, None),
        P(),
        P(("ctx", "exp"), None),
        P(("ctx", "exp"), None),
        P(("ctx", "exp"), None),
        P(("ctx", "exp"), None, None),
        P(("ctx", "exp"), None, None),
        P(("ctx", "exp"), None, None),
    )
    return jax.shard_map(
        body,
        mesh=mesh,
        in_specs=placed,
        out_specs=(P("exp", "ctx", None), P(("ctx", "exp"), None)),
        check_vma=False,
    )
```

```python
import functools

import jax
import jax.numpy as jnp
from jax import lax
from jax.experimental import pallas as pl
from jax.experimental.pallas import tpu as pltpu
from jax.sharding import PartitionSpec as P

TOP_PRECISION = lax.Precision.HIGHEST
NORM_EPSILON = 1e-06
CAPACITY = 3
LANES = 128
VMEM_BYTES = 36 * 1024 * 1024


def passed_along(block, axis, distance):
    devices = range(lax.axis_size(axis))
    route = [(i - distance, i) for i in devices if i - distance in devices]
    return lax.ppermute(block, axis, route)


def block_parts(queries, key_vectors, values, write_strength, log_fading_factor, block_inverse):
    tracks, length, head_width = queries.shape
    block_size = block_inverse.shape[-1]
    blocks = length // block_size
    shape_four = (tracks, blocks, block_size, head_width)
    query_blocks = queries.reshape(shape_four)
    key_blocks = key_vectors.reshape(shape_four)
    value_blocks = values.reshape(shape_four)
    strength = write_strength.reshape(tracks, blocks, block_size)
    running = jnp.cumsum(log_fading_factor.reshape(tracks, blocks, block_size), axis=-1)
    growth = jnp.exp(running)
    final_log = running[..., -1:]
    write_keys = jnp.einsum(
        "sbij,sbjh->sbih",
        block_inverse,
        key_blocks * (strength * growth)[..., None],
        precision=TOP_PRECISION,
    )
    write_values = jnp.einsum(
        "sbij,sbjh->sbih",
        block_inverse,
        value_blocks * strength[..., None],
        precision=TOP_PRECISION,
    )
    faded_keys = key_blocks * jnp.exp(final_log - running)[..., None]
    faded_queries = query_blocks * growth[..., None]
    row_index = lax.broadcasted_iota(jnp.int32, (block_size, block_size), 0)
    col_index = lax.broadcasted_iota(jnp.int32, (block_size, block_size), 1)
    spread = running[..., :, None] - running[..., None, :]
    causal_fade = jnp.where(row_index >= col_index, jnp.exp(jnp.minimum(spread, 0.0)), 0.0)
    causal = (
        jnp.einsum("sbih,sbjh->sbij", query_blocks, key_blocks, precision=TOP_PRECISION)
        * causal_fade
    )
    return (faded_queries, write_keys, write_values, faded_keys, causal, jnp.exp(final_log))


def block_step(states, pieces):
    faded_queries, write_keys, write_values, faded_keys, causal, decays = pieces
    fresh_values = write_values - jnp.einsum(
        "sch,shv->scv", write_keys, states, precision=TOP_PRECISION
    )
    attended = jnp.einsum("sch,shv->scv", faded_queries, states, precision=TOP_PRECISION)
    attended = attended + jnp.einsum("sij,sjv->siv", causal, fresh_values, precision=TOP_PRECISION)
    states = decays[..., None] * states + jnp.einsum(
        "sch,scv->shv", faded_keys, fresh_values, precision=TOP_PRECISION
    )
    return (states, attended)


def run_blocks(pieces, states):
    moved = tuple((jnp.moveaxis(piece_item, 1, 0) for piece_item in pieces))
    states, attended = lax.scan(block_step, states, moved)
    return (states, jnp.moveaxis(attended, 0, 1))


def gated_norm(attended, norm_gain, out_gate):
    root_mean = jnp.sqrt(jnp.mean(attended * attended, axis=-1, keepdims=True) + NORM_EPSILON)
    return attended / root_mean * norm_gain * jax.nn.silu(out_gate)


def compose(carried, block_piece):
    current_mapping, current_addend = carried
    segment_mapping, segment_addend = block_piece
    updated_mapping = jnp.einsum(
        "qfz,qze->qfe", segment_mapping, current_mapping, precision=TOP_PRECISION
    )
    updated_addend = (
        jnp.einsum("qfz,qze->qfe", segment_mapping, current_addend, precision=TOP_PRECISION)
        + segment_addend
    )
    return ((updated_mapping, updated_addend), None)


def delta_front(queries, key_vectors, values, write_strength, log_fading_factor, block_inverse):
    tracks, length, head_width = queries.shape
    pieces = block_parts(
        queries, key_vectors, values, write_strength, log_fading_factor, block_inverse
    )
    faded_queries, write_keys, write_values, faded_keys, causal, decays = pieces
    unit_matrix = jnp.eye(head_width, dtype=jnp.float32)
    identity_map = jnp.broadcast_to(unit_matrix, (tracks, head_width, head_width))
    block_maps = decays[..., None] * unit_matrix - jnp.einsum(
        "sbch,sbck->sbhk", faded_keys, write_keys, precision=TOP_PRECISION
    )
    block_adds = jnp.einsum("sbch,sbcv->sbhv", faded_keys, write_values, precision=TOP_PRECISION)
    (section_mapping, section_addend), _ = lax.scan(
        compose,
        (identity_map, jnp.zeros_like(identity_map)),
        (jnp.moveaxis(block_maps, 1, 0), jnp.moveaxis(block_adds, 1, 0)),
    )
    incoming_state = jnp.zeros_like(section_addend)
    for relay_turn in range(lax.axis_size("ctx") - 1):
        departing_state = (
            jnp.einsum("qfz,qze->qfe", section_mapping, incoming_state, precision=TOP_PRECISION)
            + section_addend
        )
        incoming_state = passed_along(departing_state.astype(jnp.bfloat16), "ctx", 1).astype(
            departing_state.dtype
        )
    return pieces, incoming_state


def named_and_rank(ranks, first, count, tokens):
    row = lax.broadcasted_iota(jnp.int32, (count, tokens), 0) + first
    named = jnp.zeros((count, tokens), jnp.bool_)
    for pick in range(ranks.shape[0]):
        named = jnp.logical_or(named, ranks[pick : pick + 1, :] == row)
    before = lax.broadcasted_iota(jnp.int32, (tokens, tokens), 0) < lax.broadcasted_iota(
        jnp.int32, (tokens, tokens), 1
    )
    earlier = jnp.dot(
        named.astype(jnp.float32).astype(jnp.bfloat16),
        before.astype(jnp.float32).astype(jnp.bfloat16),
        preferred_element_type=jnp.float32,
    )
    return named, earlier


def ranks_of(picks, owner_count, context_size):
    context = jnp.floor(picks.astype(jnp.float32) * (1.0 / owner_count)).astype(jnp.int32)
    return (picks - context * owner_count) * context_size + context


def pack_kernel(owner_count, context_size, picks_ref, hidden_ref, out_ref, spread_ref):
    tokens, width = hidden_ref.shape
    parts = width // LANES
    per = CAPACITY * parts
    count = out_ref.shape[0] // per
    ranks = ranks_of(picks_ref[...], owner_count, context_size)
    named, earlier = named_and_rank(ranks, pl.program_id(0) * count, count, tokens)
    chosen = jnp.concatenate(
        [
            jnp.where(jnp.logical_and(named, earlier == slot), 1.0, 0.0)
            for slot in range(CAPACITY)
        ],
        axis=0,
    ).astype(jnp.bfloat16)
    rows = jnp.dot(chosen, hidden_ref[...], preferred_element_type=jnp.float32)
    for slot in range(CAPACITY):
        for part in range(parts):
            spread_ref[pl.ds(slot * parts + part, count, stride=per), :] = rows[
                slot * count : (slot + 1) * count, part * LANES : (part + 1) * LANES
            ]
    out_ref[...] = spread_ref[...].astype(jnp.bfloat16)


def pack_rows(picks, hidden, owner_count, context_size, steps):
    tokens, width = hidden.shape
    experts = owner_count * context_size
    rows = experts * CAPACITY * width // LANES
    return pl.pallas_call(
        functools.partial(pack_kernel, owner_count, context_size),
        grid=(steps,),
        out_shape=pltpu.HBM((rows, LANES), jnp.bfloat16),
        in_specs=[
            pl.BlockSpec(picks.shape, lambda i: (0, 0)),
            pl.BlockSpec(hidden.shape, lambda i: (0, 0)),
        ],
        out_specs=pl.BlockSpec((rows // steps, LANES), lambda i: (i, 0)),
        scratch_shapes=[pltpu.VMEM((rows // steps, LANES), jnp.float32)],
        compiler_params=pltpu.CompilerParams(vmem_limit_bytes=VMEM_BYTES),
        cost_estimate=pl.CostEstimate(
            flops=2 * experts * CAPACITY * tokens * width, bytes_accessed=rows * 256, transcendentals=0
        ),
        name="pack_rows",
    )(
        pltpu.with_memory_space_constraint(picks, pltpu.HBM),
        pltpu.with_memory_space_constraint(hidden, pltpu.HBM),
    )


def expert_kernel(
    received_ref, gate_ref, up_ref, down_ref, out_ref, spread_ref, gate_here, up_here, down_here, ready
):
    width = gate_here.shape[0]
    parts = width // LANES
    per = CAPACITY * parts
    count = received_ref.shape[0] // per
    loads = [
        pltpu.make_async_copy(there, here, ready.at[i])
        for i, (there, here) in enumerate(
            ((gate_ref, gate_here), (up_ref, up_here), (down_ref, down_here))
        )
    ]
    first = pl.program_id(0) == 0

    @pl.when(first)
    def _():
        for load in loads:
            load.start()

    spread_ref[...] = received_ref[...].astype(jnp.float32)
    rows = jnp.concatenate(
        [
            jnp.concatenate(
                [
                    spread_ref[pl.ds(slot * parts + part, count, stride=per), :].astype(jnp.bfloat16)
                    for part in range(parts)
                ],
                axis=1,
            )
            for slot in range(CAPACITY)
        ],
        axis=0,
    )

    @pl.when(first)
    def _():
        loads[0].wait()
        loads[1].wait()

    gate = jnp.dot(rows, gate_here[...], preferred_element_type=jnp.float32)
    up = jnp.dot(rows, up_here[...], preferred_element_type=jnp.float32)
    active = (gate / (1.0 + jnp.exp(-gate)) * up).astype(jnp.bfloat16)

    @pl.when(first)
    def _():
        loads[2].wait()

    produced = jnp.dot(active, down_here[...], preferred_element_type=jnp.float32)
    for slot in range(CAPACITY):
        for part in range(parts):
            spread_ref[pl.ds(slot * parts + part, count, stride=per), :] = produced[
                slot * count : (slot + 1) * count, part * LANES : (part + 1) * LANES
            ]
    out_ref[...] = spread_ref[...].astype(jnp.bfloat16)


def expert_rows(received, gate_weights, up_weights, down_weights, steps):
    rows = received.shape[0]
    width, units = gate_weights.shape
    slots = rows * LANES // width
    block = pl.BlockSpec((rows // steps, LANES), lambda i: (i, 0))
    whole = pl.BlockSpec(memory_space=pl.ANY)
    weights = [
        pltpu.with_memory_space_constraint(weight, pltpu.HBM)
        for weight in (gate_weights, up_weights, down_weights)
    ]
    return pl.pallas_call(
        expert_kernel,
        grid=(steps,),
        out_shape=pltpu.HBM(received.shape, jnp.bfloat16),
        in_specs=[block, whole, whole, whole],
        out_specs=block,
        scratch_shapes=[
            pltpu.VMEM((rows // steps, LANES), jnp.float32),
            pltpu.VMEM(gate_weights.shape, jnp.bfloat16),
            pltpu.VMEM(up_weights.shape, jnp.bfloat16),
            pltpu.VMEM(down_weights.shape, jnp.bfloat16),
            pltpu.SemaphoreType.DMA((3,)),
        ],
        compiler_params=pltpu.CompilerParams(vmem_limit_bytes=VMEM_BYTES),
        cost_estimate=pl.CostEstimate(
            flops=6 * slots * width * units,
            bytes_accessed=4 * rows * LANES + 6 * width * units,
            transcendentals=slots * units,
        ),
        name="expert_rows",
    )(received, *weights)


def combine_kernel(owner_count, context_size, picks_ref, weights_ref, returned_ref, out_ref, spread_ref, total_ref):
    tokens, width = out_ref.shape
    parts = width // LANES
    per = CAPACITY * parts
    count = returned_ref.shape[0] // per
    step = pl.program_id(0)

    @pl.when(step == 0)
    def _():
        total_ref[...] = jnp.zeros_like(total_ref)

    spread_ref[...] = returned_ref[...].astype(jnp.float32)
    ranks = ranks_of(picks_ref[...], owner_count, context_size)
    named, earlier = named_and_rank(ranks, step * count, count, tokens)
    row = lax.broadcasted_iota(jnp.int32, (count, tokens), 0) + step * count
    scale = jnp.zeros((count, tokens), jnp.float32)
    for pick in range(ranks.shape[0]):
        scale = jnp.where(ranks[pick : pick + 1, :] == row, weights_ref[pick : pick + 1, :], scale)
    high = scale.astype(jnp.bfloat16).astype(jnp.float32)
    halves = jnp.concatenate([high, scale - high], axis=1)
    at = jnp.concatenate([jnp.where(named, earlier, -1.0)] * 2, axis=1)
    table = jnp.concatenate(
        [jnp.where(at == slot, halves, 0.0) for slot in range(CAPACITY)], axis=0
    ).astype(jnp.bfloat16)
    rows = jnp.concatenate(
        [
            jnp.concatenate(
                [
                    spread_ref[pl.ds(slot * parts + part, count, stride=per), :].astype(jnp.bfloat16)
                    for part in range(parts)
                ],
                axis=1,
            )
            for slot in range(CAPACITY)
        ],
        axis=0,
    )
    both = lax.dot_general(
        table, rows, (((0,), (0,)), ((), ())), preferred_element_type=jnp.float32
    )
    total = total_ref[...] + (both[:tokens] + both[tokens:])
    total_ref[...] = total

    @pl.when(step == pl.num_programs(0) - 1)
    def _():
        out_ref[...] = total.astype(jnp.bfloat16)


def combine_rows(picks, weights, returned, owner_count, context_size, width, steps):
    tokens = picks.shape[1]
    rows = returned.shape[0]
    return pl.pallas_call(
        functools.partial(combine_kernel, owner_count, context_size),
        grid=(steps,),
        out_shape=jax.ShapeDtypeStruct((tokens, width), jnp.bfloat16),
        in_specs=[
            pl.BlockSpec(picks.shape, lambda i: (0, 0)),
            pl.BlockSpec(weights.shape, lambda i: (0, 0)),
            pl.BlockSpec((rows // steps, LANES), lambda i: (i, 0)),
        ],
        out_specs=pl.BlockSpec((tokens, width), lambda i: (0, 0)),
        scratch_shapes=[
            pltpu.VMEM((rows // steps, LANES), jnp.float32),
            pltpu.VMEM((tokens, width), jnp.float32),
        ],
        compiler_params=pltpu.CompilerParams(vmem_limit_bytes=VMEM_BYTES),
        cost_estimate=pl.CostEstimate(
            flops=4 * rows * LANES * tokens, bytes_accessed=2 * rows * LANES, transcendentals=0
        ),
        name="combine_rows",
    )(picks, weights, returned)


def exchange(rows):
    return lax.all_to_all(rows, ("exp", "ctx"), split_axis=0, concat_axis=0, tiled=True)


def body(
    queries,
    key_vectors,
    values,
    out_gate,
    write_strength,
    log_fading_factor,
    block_inverse,
    norm_gain,
    hidden,
    routes,
    route_weights,
    gate_weights,
    up_weights,
    down_weights,
):
    width = hidden.shape[1]
    context_size = lax.axis_size("ctx")
    owner_count = lax.axis_size("exp")
    picks = routes.T
    outgoing = pack_rows(picks, hidden, owner_count, context_size, 4)
    received = exchange(outgoing)
    pieces, incoming_state = delta_front(
        queries, key_vectors, values, write_strength, log_fading_factor, block_inverse
    )
    received, incoming_state = lax.optimization_barrier((received, incoming_state))
    produced = expert_rows(received, gate_weights[0], up_weights[0], down_weights[0], 4)
    returned = exchange(produced)
    expert_output = combine_rows(
        picks, route_weights.T, returned, owner_count, context_size, width, 4
    )
    _, attended = run_blocks(pieces, incoming_state)
    mixer_output = gated_norm(attended.reshape(out_gate.shape), norm_gain, out_gate)
    return (mixer_output, expert_output)


def solution(mesh):
    placed = (
        P("exp", "ctx", None),
        P("exp", "ctx", None),
        P("exp", "ctx", None),
        P("exp", "ctx", None),
        P("exp", "ctx"),
        P("exp", "ctx"),
        P("exp", "ctx", None, None),
        P(),
        P(("ctx", "exp"), None),
        P(("ctx", "exp"), None),
        P(("ctx", "exp"), None),
        P(("ctx", "exp"), None, None),
        P(("ctx", "exp"), None, None),
        P(("ctx", "exp"), None, None),
    )
    return jax.shard_map(
        body,
        mesh=mesh,
        in_specs=placed,
        out_specs=(P("exp", "ctx", None), P(("ctx", "exp"), None)),
        check_vma=False,
    )
```

```python
import functools

import jax
import jax.numpy as jnp
from jax import lax
from jax.experimental import pallas as pl
from jax.experimental.pallas import tpu as pltpu
from jax.sharding import PartitionSpec as P

TOP_PRECISION = lax.Precision.HIGHEST
NORM_EPSILON = 1e-06
CAPACITY = 3
LANES = 128
VMEM_BYTES = 36 * 1024 * 1024


def passed_along(block, axis, distance):
    devices = range(lax.axis_size(axis))
    route = [(i - distance, i) for i in devices if i - distance in devices]
    return lax.ppermute(block, axis, route)


def block_parts(queries, key_vectors, values, write_strength, log_fading_factor, block_inverse):
    tracks, length, head_width = queries.shape
    block_size = block_inverse.shape[-1]
    blocks = length // block_size
    shape_four = (tracks, blocks, block_size, head_width)
    query_blocks = queries.reshape(shape_four)
    key_blocks = key_vectors.reshape(shape_four)
    value_blocks = values.reshape(shape_four)
    strength = write_strength.reshape(tracks, blocks, block_size)
    running = jnp.cumsum(log_fading_factor.reshape(tracks, blocks, block_size), axis=-1)
    growth = jnp.exp(running)
    final_log = running[..., -1:]
    write_keys = jnp.einsum(
        "sbij,sbjh->sbih",
        block_inverse,
        key_blocks * (strength * growth)[..., None],
        precision=TOP_PRECISION,
    )
    write_values = jnp.einsum(
        "sbij,sbjh->sbih",
        block_inverse,
        value_blocks * strength[..., None],
        precision=TOP_PRECISION,
    )
    faded_keys = key_blocks * jnp.exp(final_log - running)[..., None]
    faded_queries = query_blocks * growth[..., None]
    row_index = lax.broadcasted_iota(jnp.int32, (block_size, block_size), 0)
    col_index = lax.broadcasted_iota(jnp.int32, (block_size, block_size), 1)
    spread = running[..., :, None] - running[..., None, :]
    causal_fade = jnp.where(row_index >= col_index, jnp.exp(jnp.minimum(spread, 0.0)), 0.0)
    causal = (
        jnp.einsum("sbih,sbjh->sbij", query_blocks, key_blocks, precision=TOP_PRECISION)
        * causal_fade
    )
    return (faded_queries, write_keys, write_values, faded_keys, causal, jnp.exp(final_log))


def block_step(states, pieces):
    faded_queries, write_keys, write_values, faded_keys, causal, decays = pieces
    fresh_values = write_values - jnp.einsum(
        "sch,shv->scv", write_keys, states, precision=TOP_PRECISION
    )
    attended = jnp.einsum("sch,shv->scv", faded_queries, states, precision=TOP_PRECISION)
    attended = attended + jnp.einsum("sij,sjv->siv", causal, fresh_values, precision=TOP_PRECISION)
    states = decays[..., None] * states + jnp.einsum(
        "sch,scv->shv", faded_keys, fresh_values, precision=TOP_PRECISION
    )
    return (states, attended)


def run_blocks(pieces, states):
    moved = tuple((jnp.moveaxis(piece_item, 1, 0) for piece_item in pieces))
    states, attended = lax.scan(block_step, states, moved)
    return (states, jnp.moveaxis(attended, 0, 1))


def gated_norm(attended, norm_gain, out_gate):
    root_mean = jnp.sqrt(jnp.mean(attended * attended, axis=-1, keepdims=True) + NORM_EPSILON)
    return attended / root_mean * norm_gain * jax.nn.silu(out_gate)


def compose(carried, block_piece):
    current_mapping, current_addend = carried
    segment_mapping, segment_addend = block_piece
    updated_mapping = jnp.einsum(
        "qfz,qze->qfe", segment_mapping, current_mapping, precision=TOP_PRECISION
    )
    updated_addend = (
        jnp.einsum("qfz,qze->qfe", segment_mapping, current_addend, precision=TOP_PRECISION)
        + segment_addend
    )
    return ((updated_mapping, updated_addend), None)


def delta_front(queries, key_vectors, values, write_strength, log_fading_factor, block_inverse):
    tracks, length, head_width = queries.shape
    pieces = block_parts(
        queries, key_vectors, values, write_strength, log_fading_factor, block_inverse
    )
    faded_queries, write_keys, write_values, faded_keys, causal, decays = pieces
    unit_matrix = jnp.eye(head_width, dtype=jnp.float32)
    identity_map = jnp.broadcast_to(unit_matrix, (tracks, head_width, head_width))
    block_maps = decays[..., None] * unit_matrix - jnp.einsum(
        "sbch,sbck->sbhk", faded_keys, write_keys, precision=TOP_PRECISION
    )
    block_adds = jnp.einsum("sbch,sbcv->sbhv", faded_keys, write_values, precision=TOP_PRECISION)
    (section_mapping, section_addend), _ = lax.scan(
        compose,
        (identity_map, jnp.zeros_like(identity_map)),
        (jnp.moveaxis(block_maps, 1, 0), jnp.moveaxis(block_adds, 1, 0)),
    )
    incoming_state = jnp.zeros_like(section_addend)
    for relay_turn in range(lax.axis_size("ctx") - 1):
        departing_state = (
            jnp.einsum("qfz,qze->qfe", section_mapping, incoming_state, precision=TOP_PRECISION)
            + section_addend
        )
        incoming_state = passed_along(departing_state.astype(jnp.bfloat16), "ctx", 1).astype(
            departing_state.dtype
        )
    return pieces, incoming_state


def named_and_rank(ranks, first, count, tokens):
    row = lax.broadcasted_iota(jnp.int32, (count, tokens), 0) + first
    named = jnp.zeros((count, tokens), jnp.bool_)
    for pick in range(ranks.shape[0]):
        named = jnp.logical_or(named, ranks[pick : pick + 1, :] == row)
    before = lax.broadcasted_iota(jnp.int32, (tokens, tokens), 0) < lax.broadcasted_iota(
        jnp.int32, (tokens, tokens), 1
    )
    earlier = jnp.dot(
        named.astype(jnp.float32).astype(jnp.bfloat16),
        before.astype(jnp.float32).astype(jnp.bfloat16),
        preferred_element_type=jnp.float32,
    )
    return named, earlier


def ranks_of(picks, owner_count, context_size):
    context = jnp.floor(picks.astype(jnp.float32) * (1.0 / owner_count)).astype(jnp.int32)
    return (picks - context * owner_count) * context_size + context


def pack_kernel(
    owner_count, context_size, blocks, picks_ref, hidden_ref, out_ref, spread_ref, result_ref, sent
):
    tokens, width = hidden_ref.shape
    parts = width // LANES
    per = CAPACITY * parts
    block = out_ref.shape[0] // blocks
    count = block // per
    ranks = ranks_of(picks_ref[...], owner_count, context_size)
    moves = []
    for i in range(blocks):
        named, earlier = named_and_rank(ranks, i * count, count, tokens)
        chosen = jnp.concatenate(
            [
                jnp.where(jnp.logical_and(named, earlier == slot), 1.0, 0.0)
                for slot in range(CAPACITY)
            ],
            axis=0,
        ).astype(jnp.bfloat16)
        rows = jnp.dot(chosen, hidden_ref[...], preferred_element_type=jnp.float32)
        for slot in range(CAPACITY):
            for part in range(parts):
                spread_ref[i, pl.ds(slot * parts + part, count, stride=per), :] = rows[
                    slot * count : (slot + 1) * count, part * LANES : (part + 1) * LANES
                ]
        result_ref[i] = spread_ref[i].astype(jnp.bfloat16)
        move = pltpu.make_async_copy(
            result_ref.at[i], out_ref.at[pl.ds(i * block, block), :], sent.at[i]
        )
        move.start()
        moves.append(move)
    for move in moves:
        move.wait()


def pack_rows(picks, hidden, owner_count, context_size, blocks):
    tokens, width = hidden.shape
    experts = owner_count * context_size
    rows = experts * CAPACITY * width // LANES
    here = pl.BlockSpec(memory_space=pltpu.VMEM)
    return pl.pallas_call(
        functools.partial(pack_kernel, owner_count, context_size, blocks),
        out_shape=pltpu.HBM((rows, LANES), jnp.bfloat16),
        in_specs=[here, here],
        out_specs=pl.BlockSpec(memory_space=pl.ANY),
        scratch_shapes=[
            pltpu.VMEM((blocks, rows // blocks, LANES), jnp.float32),
            pltpu.VMEM((blocks, rows // blocks, LANES), jnp.bfloat16),
            pltpu.SemaphoreType.DMA((blocks,)),
        ],
        compiler_params=pltpu.CompilerParams(vmem_limit_bytes=VMEM_BYTES),
        cost_estimate=pl.CostEstimate(
            flops=2 * experts * CAPACITY * tokens * width, bytes_accessed=rows * 256, transcendentals=0
        ),
        name="pack_rows",
    )(
        pltpu.with_memory_space_constraint(picks, pltpu.HBM),
        pltpu.with_memory_space_constraint(hidden, pltpu.HBM),
    )


def expert_kernel(
    blocks,
    received_ref,
    gate_ref,
    up_ref,
    down_ref,
    out_ref,
    spread_ref,
    result_ref,
    gate_here,
    up_here,
    down_here,
    ready,
    sent,
):
    width = gate_here.shape[0]
    parts = width // LANES
    per = CAPACITY * parts
    block = received_ref.shape[0] // blocks
    count = block // per
    loads = [
        pltpu.make_async_copy(there, here, ready.at[i])
        for i, (there, here) in enumerate(
            ((gate_ref, gate_here), (up_ref, up_here), (down_ref, down_here))
        )
    ]
    for load in loads:
        load.start()

    def unpacked(i):
        spread_ref[i] = received_ref[pl.ds(i * block, block), :].astype(jnp.float32)
        return jnp.concatenate(
            [
                jnp.concatenate(
                    [
                        spread_ref[i, pl.ds(slot * parts + part, count, stride=per), :].astype(
                            jnp.bfloat16
                        )
                        for part in range(parts)
                    ],
                    axis=1,
                )
                for slot in range(CAPACITY)
            ],
            axis=0,
        )

    rows = unpacked(0)
    moves = []
    for i in range(blocks):
        if i == 0:
            loads[0].wait()
        gate = jnp.dot(rows, gate_here[...], preferred_element_type=jnp.float32)
        if i == 0:
            loads[1].wait()
            loads[2].wait()
        up = jnp.dot(rows, up_here[...], preferred_element_type=jnp.float32)
        if i + 1 < blocks:
            rows = unpacked(i + 1)
        active = (gate / (1.0 + jnp.exp(-gate)) * up).astype(jnp.bfloat16)
        produced = jnp.dot(active, down_here[...], preferred_element_type=jnp.float32)
        for slot in range(CAPACITY):
            for part in range(parts):
                spread_ref[i, pl.ds(slot * parts + part, count, stride=per), :] = produced[
                    slot * count : (slot + 1) * count, part * LANES : (part + 1) * LANES
                ]
        for half in range(2):
            at = pl.ds(half * (block // 2), block // 2)
            result_ref[i, at, :] = spread_ref[i, at, :].astype(jnp.bfloat16)
            move = pltpu.make_async_copy(
                result_ref.at[i, at, :],
                out_ref.at[pl.ds(i * block + half * (block // 2), block // 2), :],
                sent.at[2 * i + half],
            )
            move.start()
            moves.append(move)
    for move in moves:
        move.wait()


def expert_rows(received, gate_weights, up_weights, down_weights, blocks):
    rows = received.shape[0]
    width, units = gate_weights.shape
    slots = rows * LANES // width
    whole = pl.BlockSpec(memory_space=pl.ANY)
    weights = [
        pltpu.with_memory_space_constraint(weight, pltpu.HBM)
        for weight in (gate_weights, up_weights, down_weights)
    ]
    return pl.pallas_call(
        functools.partial(expert_kernel, blocks),
        out_shape=pltpu.HBM(received.shape, jnp.bfloat16),
        in_specs=[pl.BlockSpec(memory_space=pltpu.VMEM), whole, whole, whole],
        out_specs=whole,
        scratch_shapes=[
            pltpu.VMEM((blocks, rows // blocks, LANES), jnp.float32),
            pltpu.VMEM((blocks, rows // blocks, LANES), jnp.bfloat16),
            pltpu.VMEM(gate_weights.shape, jnp.bfloat16),
            pltpu.VMEM(up_weights.shape, jnp.bfloat16),
            pltpu.VMEM(down_weights.shape, jnp.bfloat16),
            pltpu.SemaphoreType.DMA((3,)),
            pltpu.SemaphoreType.DMA((2 * blocks,)),
        ],
        compiler_params=pltpu.CompilerParams(vmem_limit_bytes=VMEM_BYTES),
        cost_estimate=pl.CostEstimate(
            flops=6 * slots * width * units,
            bytes_accessed=4 * rows * LANES + 6 * width * units,
            transcendentals=slots * units,
        ),
        name="expert_rows",
    )(received, *weights)


def combine_kernel(owner_count, context_size, picks_ref, weights_ref, returned_ref, out_ref, spread_ref, total_ref):
    tokens, width = out_ref.shape
    parts = width // LANES
    per = CAPACITY * parts
    count = returned_ref.shape[0] // per
    step = pl.program_id(0)

    @pl.when(step == 0)
    def _():
        total_ref[...] = jnp.zeros_like(total_ref)

    spread_ref[...] = returned_ref[...].astype(jnp.float32)
    ranks = ranks_of(picks_ref[...], owner_count, context_size)
    named, earlier = named_and_rank(ranks, step * count, count, tokens)
    row = lax.broadcasted_iota(jnp.int32, (count, tokens), 0) + step * count
    scale = jnp.zeros((count, tokens), jnp.float32)
    for pick in range(ranks.shape[0]):
        scale = jnp.where(ranks[pick : pick + 1, :] == row, weights_ref[pick : pick + 1, :], scale)
    high = scale.astype(jnp.bfloat16).astype(jnp.float32)
    halves = jnp.concatenate([high, scale - high], axis=1)
    at = jnp.concatenate([jnp.where(named, earlier, -1.0)] * 2, axis=1)
    table = jnp.concatenate(
        [jnp.where(at == slot, halves, 0.0) for slot in range(CAPACITY)], axis=0
    ).astype(jnp.bfloat16)
    rows = jnp.concatenate(
        [
            jnp.concatenate(
                [
                    spread_ref[pl.ds(slot * parts + part, count, stride=per), :].astype(jnp.bfloat16)
                    for part in range(parts)
                ],
                axis=1,
            )
            for slot in range(CAPACITY)
        ],
        axis=0,
    )
    both = lax.dot_general(
        table, rows, (((0,), (0,)), ((), ())), preferred_element_type=jnp.float32
    )
    total = total_ref[...] + (both[:tokens] + both[tokens:])
    total_ref[...] = total

    @pl.when(step == pl.num_programs(0) - 1)
    def _():
        out_ref[...] = total.astype(jnp.bfloat16)


def combine_rows(picks, weights, returned, owner_count, context_size, width, steps):
    tokens = picks.shape[1]
    rows = returned.shape[0]
    return pl.pallas_call(
        functools.partial(combine_kernel, owner_count, context_size),
        grid=(steps,),
        out_shape=jax.ShapeDtypeStruct((tokens, width), jnp.bfloat16),
        in_specs=[
            pl.BlockSpec(picks.shape, lambda i: (0, 0)),
            pl.BlockSpec(weights.shape, lambda i: (0, 0)),
            pl.BlockSpec((rows // steps, LANES), lambda i: (i, 0)),
        ],
        out_specs=pl.BlockSpec((tokens, width), lambda i: (0, 0)),
        scratch_shapes=[
            pltpu.VMEM((rows // steps, LANES), jnp.float32),
            pltpu.VMEM((tokens, width), jnp.float32),
        ],
        compiler_params=pltpu.CompilerParams(vmem_limit_bytes=VMEM_BYTES),
        cost_estimate=pl.CostEstimate(
            flops=4 * rows * LANES * tokens, bytes_accessed=2 * rows * LANES, transcendentals=0
        ),
        name="combine_rows",
    )(picks, weights, returned)


def exchange(rows):
    return lax.all_to_all(rows, ("exp", "ctx"), split_axis=0, concat_axis=0, tiled=True)


def body(
    queries,
    key_vectors,
    values,
    out_gate,
    write_strength,
    log_fading_factor,
    block_inverse,
    norm_gain,
    hidden,
    routes,
    route_weights,
    gate_weights,
    up_weights,
    down_weights,
):
    width = hidden.shape[1]
    context_size = lax.axis_size("ctx")
    owner_count = lax.axis_size("exp")
    picks = routes.T
    outgoing = pack_rows(picks, hidden, owner_count, context_size, 4)
    received = exchange(outgoing)
    pieces, incoming_state = delta_front(
        queries, key_vectors, values, write_strength, log_fading_factor, block_inverse
    )
    received, incoming_state = lax.optimization_barrier((received, incoming_state))
    produced = expert_rows(received, gate_weights[0], up_weights[0], down_weights[0], 4)
    returned = exchange(produced)
    expert_output = combine_rows(
        picks, route_weights.T, returned, owner_count, context_size, width, 1
    )
    _, attended = run_blocks(pieces, incoming_state)
    mixer_output = gated_norm(attended.reshape(out_gate.shape), norm_gain, out_gate)
    return (mixer_output, expert_output)


def solution(mesh):
    placed = (
        P("exp", "ctx", None),
        P("exp", "ctx", None),
        P("exp", "ctx", None),
        P("exp", "ctx", None),
        P("exp", "ctx"),
        P("exp", "ctx"),
        P("exp", "ctx", None, None),
        P(),
        P(("ctx", "exp"), None),
        P(("ctx", "exp"), None),
        P(("ctx", "exp"), None),
        P(("ctx", "exp"), None, None),
        P(("ctx", "exp"), None, None),
        P(("ctx", "exp"), None, None),
    )
    return jax.shard_map(
        body,
        mesh=mesh,
        in_specs=placed,
        out_specs=(P("exp", "ctx", None), P(("ctx", "exp"), None)),
        check_vma=False,
    )
```

```python
import functools

import jax
import jax.numpy as jnp
from jax import lax
from jax.experimental import pallas as pl
from jax.experimental.pallas import tpu as pltpu
from jax.sharding import PartitionSpec as P

TOP_PRECISION = lax.Precision.HIGHEST
NORM_EPSILON = 1e-06
CAPACITY = 3
LANES = 128
VMEM_BYTES = 36 * 1024 * 1024


def passed_along(block, axis, distance):
    devices = range(lax.axis_size(axis))
    route = [(i - distance, i) for i in devices if i - distance in devices]
    return lax.ppermute(block, axis, route)


def block_parts(queries, key_vectors, values, write_strength, log_fading_factor, block_inverse):
    tracks, length, head_width = queries.shape
    block_size = block_inverse.shape[-1]
    blocks = length // block_size
    shape_four = (tracks, blocks, block_size, head_width)
    query_blocks = queries.reshape(shape_four)
    key_blocks = key_vectors.reshape(shape_four)
    value_blocks = values.reshape(shape_four)
    strength = write_strength.reshape(tracks, blocks, block_size)
    running = jnp.cumsum(log_fading_factor.reshape(tracks, blocks, block_size), axis=-1)
    growth = jnp.exp(running)
    final_log = running[..., -1:]
    write_keys = jnp.einsum(
        "sbij,sbjh->sbih",
        block_inverse,
        key_blocks * (strength * growth)[..., None],
        precision=TOP_PRECISION,
    )
    write_values = jnp.einsum(
        "sbij,sbjh->sbih",
        block_inverse,
        value_blocks * strength[..., None],
        precision=TOP_PRECISION,
    )
    faded_keys = key_blocks * jnp.exp(final_log - running)[..., None]
    faded_queries = query_blocks * growth[..., None]
    row_index = lax.broadcasted_iota(jnp.int32, (block_size, block_size), 0)
    col_index = lax.broadcasted_iota(jnp.int32, (block_size, block_size), 1)
    spread = running[..., :, None] - running[..., None, :]
    causal_fade = jnp.where(row_index >= col_index, jnp.exp(jnp.minimum(spread, 0.0)), 0.0)
    causal = (
        jnp.einsum("sbih,sbjh->sbij", query_blocks, key_blocks, precision=TOP_PRECISION)
        * causal_fade
    )
    return (faded_queries, write_keys, write_values, faded_keys, causal, jnp.exp(final_log))


def block_step(states, pieces):
    faded_queries, write_keys, write_values, faded_keys, causal, decays = pieces
    fresh_values = write_values - jnp.einsum(
        "sch,shv->scv", write_keys, states, precision=TOP_PRECISION
    )
    attended = jnp.einsum("sch,shv->scv", faded_queries, states, precision=TOP_PRECISION)
    attended = attended + jnp.einsum("sij,sjv->siv", causal, fresh_values, precision=TOP_PRECISION)
    states = decays[..., None] * states + jnp.einsum(
        "sch,scv->shv", faded_keys, fresh_values, precision=TOP_PRECISION
    )
    return (states, attended)


def run_blocks(pieces, states):
    moved = tuple((jnp.moveaxis(piece_item, 1, 0) for piece_item in pieces))
    states, attended = lax.scan(block_step, states, moved)
    return (states, jnp.moveaxis(attended, 0, 1))


def gated_norm(attended, norm_gain, out_gate):
    root_mean = jnp.sqrt(jnp.mean(attended * attended, axis=-1, keepdims=True) + NORM_EPSILON)
    return attended / root_mean * norm_gain * jax.nn.silu(out_gate)


def compose(carried, block_piece):
    current_mapping, current_addend = carried
    segment_mapping, segment_addend = block_piece
    updated_mapping = jnp.einsum(
        "qfz,qze->qfe", segment_mapping, current_mapping, precision=TOP_PRECISION
    )
    updated_addend = (
        jnp.einsum("qfz,qze->qfe", segment_mapping, current_addend, precision=TOP_PRECISION)
        + segment_addend
    )
    return ((updated_mapping, updated_addend), None)


def delta_front(queries, key_vectors, values, write_strength, log_fading_factor, block_inverse):
    tracks, length, head_width = queries.shape
    pieces = block_parts(
        queries, key_vectors, values, write_strength, log_fading_factor, block_inverse
    )
    faded_queries, write_keys, write_values, faded_keys, causal, decays = pieces
    unit_matrix = jnp.eye(head_width, dtype=jnp.float32)
    identity_map = jnp.broadcast_to(unit_matrix, (tracks, head_width, head_width))
    block_maps = decays[..., None] * unit_matrix - jnp.einsum(
        "sbch,sbck->sbhk", faded_keys, write_keys, precision=TOP_PRECISION
    )
    block_adds = jnp.einsum("sbch,sbcv->sbhv", faded_keys, write_values, precision=TOP_PRECISION)
    (section_mapping, section_addend), _ = lax.scan(
        compose,
        (identity_map, jnp.zeros_like(identity_map)),
        (jnp.moveaxis(block_maps, 1, 0), jnp.moveaxis(block_adds, 1, 0)),
    )
    incoming_state = jnp.zeros_like(section_addend)
    for relay_turn in range(lax.axis_size("ctx") - 1):
        departing_state = (
            jnp.einsum("qfz,qze->qfe", section_mapping, incoming_state, precision=TOP_PRECISION)
            + section_addend
        )
        incoming_state = passed_along(departing_state.astype(jnp.bfloat16), "ctx", 1).astype(
            departing_state.dtype
        )
    return pieces, incoming_state


def named_and_rank(ranks, first, count, tokens):
    row = lax.broadcasted_iota(jnp.int32, (count, tokens), 0) + first
    named = jnp.zeros((count, tokens), jnp.bool_)
    for pick in range(ranks.shape[0]):
        named = jnp.logical_or(named, ranks[pick : pick + 1, :] == row)
    before = lax.broadcasted_iota(jnp.int32, (tokens, tokens), 0) < lax.broadcasted_iota(
        jnp.int32, (tokens, tokens), 1
    )
    earlier = jnp.dot(
        named.astype(jnp.float32).astype(jnp.bfloat16),
        before.astype(jnp.float32).astype(jnp.bfloat16),
        preferred_element_type=jnp.float32,
    )
    return named, earlier


def ranks_of(picks, owner_count, context_size):
    context = jnp.floor(picks.astype(jnp.float32) * (1.0 / owner_count)).astype(jnp.int32)
    return (picks - context * owner_count) * context_size + context


def pack_kernel(
    owner_count, context_size, blocks, picks_ref, hidden_ref, out_ref, spread_ref, result_ref, sent
):
    tokens, width = hidden_ref.shape
    parts = width // LANES
    per = CAPACITY * parts
    block = out_ref.shape[0] // blocks
    count = block // per
    ranks = ranks_of(picks_ref[...], owner_count, context_size)
    moves = []
    for i in range(blocks):
        named, earlier = named_and_rank(ranks, i * count, count, tokens)
        chosen = jnp.concatenate(
            [
                jnp.where(jnp.logical_and(named, earlier == slot), 1.0, 0.0)
                for slot in range(CAPACITY)
            ],
            axis=0,
        ).astype(jnp.bfloat16)
        rows = jnp.dot(chosen, hidden_ref[...], preferred_element_type=jnp.float32)
        for slot in range(CAPACITY):
            for part in range(parts):
                spread_ref[i, pl.ds(slot * parts + part, count, stride=per), :] = rows[
                    slot * count : (slot + 1) * count, part * LANES : (part + 1) * LANES
                ]
        result_ref[i] = spread_ref[i].astype(jnp.bfloat16)
        move = pltpu.make_async_copy(
            result_ref.at[i], out_ref.at[pl.ds(i * block, block), :], sent.at[i]
        )
        move.start()
        moves.append(move)
    for move in moves:
        move.wait()


def pack_rows(picks, hidden, owner_count, context_size, blocks):
    tokens, width = hidden.shape
    experts = owner_count * context_size
    rows = experts * CAPACITY * width // LANES
    here = pl.BlockSpec(memory_space=pltpu.VMEM)
    return pl.pallas_call(
        functools.partial(pack_kernel, owner_count, context_size, blocks),
        out_shape=pltpu.HBM((rows, LANES), jnp.bfloat16),
        in_specs=[here, here],
        out_specs=pl.BlockSpec(memory_space=pl.ANY),
        scratch_shapes=[
            pltpu.VMEM((blocks, rows // blocks, LANES), jnp.float32),
            pltpu.VMEM((blocks, rows // blocks, LANES), jnp.bfloat16),
            pltpu.SemaphoreType.DMA((blocks,)),
        ],
        compiler_params=pltpu.CompilerParams(vmem_limit_bytes=VMEM_BYTES),
        cost_estimate=pl.CostEstimate(
            flops=2 * experts * CAPACITY * tokens * width, bytes_accessed=rows * 256, transcendentals=0
        ),
        name="pack_rows",
    )(
        pltpu.with_memory_space_constraint(picks, pltpu.HBM),
        pltpu.with_memory_space_constraint(hidden, pltpu.HBM),
    )


def staging_kernel(*refs):
    count = len(refs) // 2
    ready = refs[-1]
    moves = [
        pltpu.make_async_copy(refs[i], refs[count + i], ready.at[i]) for i in range(count)
    ]
    for move in moves:
        move.start()
    for move in moves:
        move.wait()


def staged(arrays):
    there = pl.BlockSpec(memory_space=pl.ANY)
    here = pl.BlockSpec(memory_space=pltpu.VMEM)
    return pl.pallas_call(
        staging_kernel,
        out_shape=[pltpu.VMEM(array.shape, array.dtype) for array in arrays],
        in_specs=[there] * len(arrays),
        out_specs=[here] * len(arrays),
        scratch_shapes=[pltpu.SemaphoreType.DMA((len(arrays),))],
        cost_estimate=pl.CostEstimate(
            flops=0, bytes_accessed=4 * sum(array.size for array in arrays), transcendentals=0
        ),
        name="staged_weights",
    )(*[pltpu.with_memory_space_constraint(array, pltpu.HBM) for array in arrays])


def expert_kernel(
    blocks,
    received_ref,
    gate_here,
    up_here,
    down_here,
    out_ref,
    spread_ref,
    result_ref,
    sent,
):
    width = gate_here.shape[0]
    parts = width // LANES
    per = CAPACITY * parts
    block = received_ref.shape[0] // blocks
    count = block // per
    def unpacked(i):
        spread_ref[i] = received_ref[pl.ds(i * block, block), :].astype(jnp.float32)
        return jnp.concatenate(
            [
                jnp.concatenate(
                    [
                        spread_ref[i, pl.ds(slot * parts + part, count, stride=per), :].astype(
                            jnp.bfloat16
                        )
                        for part in range(parts)
                    ],
                    axis=1,
                )
                for slot in range(CAPACITY)
            ],
            axis=0,
        )

    rows = unpacked(0)
    moves = []
    for i in range(blocks):
        gate = jnp.dot(rows, gate_here[...], preferred_element_type=jnp.float32)
        up = jnp.dot(rows, up_here[...], preferred_element_type=jnp.float32)
        if i + 1 < blocks:
            rows = unpacked(i + 1)
        active = (gate / (1.0 + jnp.exp(-gate)) * up).astype(jnp.bfloat16)
        produced = jnp.dot(active, down_here[...], preferred_element_type=jnp.float32)
        for slot in range(CAPACITY):
            for part in range(parts):
                spread_ref[i, pl.ds(slot * parts + part, count, stride=per), :] = produced[
                    slot * count : (slot + 1) * count, part * LANES : (part + 1) * LANES
                ]
        for half in range(2):
            at = pl.ds(half * (block // 2), block // 2)
            result_ref[i, at, :] = spread_ref[i, at, :].astype(jnp.bfloat16)
            move = pltpu.make_async_copy(
                result_ref.at[i, at, :],
                out_ref.at[pl.ds(i * block + half * (block // 2), block // 2), :],
                sent.at[2 * i + half],
            )
            move.start()
            moves.append(move)
    for move in moves:
        move.wait()


def expert_rows(received, gate_weights, up_weights, down_weights, blocks):
    rows = received.shape[0]
    width, units = gate_weights.shape
    slots = rows * LANES // width
    whole = pl.BlockSpec(memory_space=pl.ANY)
    here = pl.BlockSpec(memory_space=pltpu.VMEM)
    return pl.pallas_call(
        functools.partial(expert_kernel, blocks),
        out_shape=pltpu.HBM(received.shape, jnp.bfloat16),
        in_specs=[here] * 4,
        out_specs=whole,
        scratch_shapes=[
            pltpu.VMEM((blocks, rows // blocks, LANES), jnp.float32),
            pltpu.VMEM((blocks, rows // blocks, LANES), jnp.bfloat16),
            pltpu.SemaphoreType.DMA((2 * blocks,)),
        ],
        compiler_params=pltpu.CompilerParams(vmem_limit_bytes=VMEM_BYTES),
        cost_estimate=pl.CostEstimate(
            flops=6 * slots * width * units,
            bytes_accessed=4 * rows * LANES + 6 * width * units,
            transcendentals=slots * units,
        ),
        name="expert_rows",
    )(received, gate_weights, up_weights, down_weights)


def combine_kernel(owner_count, context_size, picks_ref, weights_ref, returned_ref, out_ref, spread_ref, total_ref):
    tokens, width = out_ref.shape
    parts = width // LANES
    per = CAPACITY * parts
    count = returned_ref.shape[0] // per
    step = pl.program_id(0)

    @pl.when(step == 0)
    def _():
        total_ref[...] = jnp.zeros_like(total_ref)

    spread_ref[...] = returned_ref[...].astype(jnp.float32)
    ranks = ranks_of(picks_ref[...], owner_count, context_size)
    named, earlier = named_and_rank(ranks, step * count, count, tokens)
    row = lax.broadcasted_iota(jnp.int32, (count, tokens), 0) + step * count
    scale = jnp.zeros((count, tokens), jnp.float32)
    for pick in range(ranks.shape[0]):
        scale = jnp.where(ranks[pick : pick + 1, :] == row, weights_ref[pick : pick + 1, :], scale)
    high = scale.astype(jnp.bfloat16).astype(jnp.float32)
    halves = jnp.concatenate([high, scale - high], axis=1)
    at = jnp.concatenate([jnp.where(named, earlier, -1.0)] * 2, axis=1)
    table = jnp.concatenate(
        [jnp.where(at == slot, halves, 0.0) for slot in range(CAPACITY)], axis=0
    ).astype(jnp.bfloat16)
    rows = jnp.concatenate(
        [
            jnp.concatenate(
                [
                    spread_ref[pl.ds(slot * parts + part, count, stride=per), :].astype(jnp.bfloat16)
                    for part in range(parts)
                ],
                axis=1,
            )
            for slot in range(CAPACITY)
        ],
        axis=0,
    )
    both = lax.dot_general(
        table, rows, (((0,), (0,)), ((), ())), preferred_element_type=jnp.float32
    )
    total = total_ref[...] + (both[:tokens] + both[tokens:])
    total_ref[...] = total

    @pl.when(step == pl.num_programs(0) - 1)
    def _():
        out_ref[...] = total.astype(jnp.bfloat16)


def combine_rows(picks, weights, returned, owner_count, context_size, width, steps):
    tokens = picks.shape[1]
    rows = returned.shape[0]
    return pl.pallas_call(
        functools.partial(combine_kernel, owner_count, context_size),
        grid=(steps,),
        out_shape=jax.ShapeDtypeStruct((tokens, width), jnp.bfloat16),
        in_specs=[
            pl.BlockSpec(picks.shape, lambda i: (0, 0)),
            pl.BlockSpec(weights.shape, lambda i: (0, 0)),
            pl.BlockSpec((rows // steps, LANES), lambda i: (i, 0)),
        ],
        out_specs=pl.BlockSpec((tokens, width), lambda i: (0, 0)),
        scratch_shapes=[
            pltpu.VMEM((rows // steps, LANES), jnp.float32),
            pltpu.VMEM((tokens, width), jnp.float32),
        ],
        compiler_params=pltpu.CompilerParams(vmem_limit_bytes=VMEM_BYTES),
        cost_estimate=pl.CostEstimate(
            flops=4 * rows * LANES * tokens, bytes_accessed=2 * rows * LANES, transcendentals=0
        ),
        name="combine_rows",
    )(picks, weights, returned)


def exchange(rows):
    return lax.all_to_all(rows, ("exp", "ctx"), split_axis=0, concat_axis=0, tiled=True)


def body(
    queries,
    key_vectors,
    values,
    out_gate,
    write_strength,
    log_fading_factor,
    block_inverse,
    norm_gain,
    hidden,
    routes,
    route_weights,
    gate_weights,
    up_weights,
    down_weights,
):
    width = hidden.shape[1]
    context_size = lax.axis_size("ctx")
    owner_count = lax.axis_size("exp")
    picks = routes.T
    outgoing = pack_rows(picks, hidden, owner_count, context_size, 4)
    received = exchange(outgoing)
    pieces, incoming_state = delta_front(
        queries, key_vectors, values, write_strength, log_fading_factor, block_inverse
    )
    weights = staged([gate_weights[0], up_weights[0], down_weights[0]])
    received, incoming_state, weights = lax.optimization_barrier(
        (received, incoming_state, weights)
    )
    produced = expert_rows(received, *weights, 4)
    returned = exchange(produced)
    expert_output = combine_rows(
        picks, route_weights.T, returned, owner_count, context_size, width, 1
    )
    _, attended = run_blocks(pieces, incoming_state)
    mixer_output = gated_norm(attended.reshape(out_gate.shape), norm_gain, out_gate)
    return (mixer_output, expert_output)


def solution(mesh):
    placed = (
        P("exp", "ctx", None),
        P("exp", "ctx", None),
        P("exp", "ctx", None),
        P("exp", "ctx", None),
        P("exp", "ctx"),
        P("exp", "ctx"),
        P("exp", "ctx", None, None),
        P(),
        P(("ctx", "exp"), None),
        P(("ctx", "exp"), None),
        P(("ctx", "exp"), None),
        P(("ctx", "exp"), None, None),
        P(("ctx", "exp"), None, None),
        P(("ctx", "exp"), None, None),
    )
    return jax.shard_map(
        body,
        mesh=mesh,
        in_specs=placed,
        out_specs=(P("exp", "ctx", None), P(("ctx", "exp"), None)),
        check_vma=False,
    )
```

```python
import functools

import jax
import jax.numpy as jnp
from jax import lax
from jax.experimental import pallas as pl
from jax.experimental.pallas import tpu as pltpu
from jax.sharding import PartitionSpec as P

TOP_PRECISION = lax.Precision.HIGHEST
NORM_EPSILON = 1e-06
CAPACITY = 3
LANES = 128
VMEM_BYTES = 36 * 1024 * 1024


def passed_along(block, axis, distance):
    devices = range(lax.axis_size(axis))
    route = [(i - distance, i) for i in devices if i - distance in devices]
    return lax.ppermute(block, axis, route)


def block_parts(queries, key_vectors, values, write_strength, log_fading_factor, block_inverse):
    tracks, length, head_width = queries.shape
    block_size = block_inverse.shape[-1]
    blocks = length // block_size
    shape_four = (tracks, blocks, block_size, head_width)
    query_blocks = queries.reshape(shape_four)
    key_blocks = key_vectors.reshape(shape_four)
    value_blocks = values.reshape(shape_four)
    strength = write_strength.reshape(tracks, blocks, block_size)
    running = jnp.cumsum(log_fading_factor.reshape(tracks, blocks, block_size), axis=-1)
    growth = jnp.exp(running)
    final_log = running[..., -1:]
    write_keys = jnp.einsum(
        "sbij,sbjh->sbih",
        block_inverse,
        key_blocks * (strength * growth)[..., None],
        precision=TOP_PRECISION,
    )
    write_values = jnp.einsum(
        "sbij,sbjh->sbih",
        block_inverse,
        value_blocks * strength[..., None],
        precision=TOP_PRECISION,
    )
    faded_keys = key_blocks * jnp.exp(final_log - running)[..., None]
    faded_queries = query_blocks * growth[..., None]
    row_index = lax.broadcasted_iota(jnp.int32, (block_size, block_size), 0)
    col_index = lax.broadcasted_iota(jnp.int32, (block_size, block_size), 1)
    spread = running[..., :, None] - running[..., None, :]
    causal_fade = jnp.where(row_index >= col_index, jnp.exp(jnp.minimum(spread, 0.0)), 0.0)
    causal = (
        jnp.einsum("sbih,sbjh->sbij", query_blocks, key_blocks, precision=TOP_PRECISION)
        * causal_fade
    )
    return (faded_queries, write_keys, write_values, faded_keys, causal, jnp.exp(final_log))


def block_step(states, pieces):
    faded_queries, write_keys, write_values, faded_keys, causal, decays = pieces
    fresh_values = write_values - jnp.einsum(
        "sch,shv->scv", write_keys, states, precision=TOP_PRECISION
    )
    attended = jnp.einsum("sch,shv->scv", faded_queries, states, precision=TOP_PRECISION)
    attended = attended + jnp.einsum("sij,sjv->siv", causal, fresh_values, precision=TOP_PRECISION)
    states = decays[..., None] * states + jnp.einsum(
        "sch,scv->shv", faded_keys, fresh_values, precision=TOP_PRECISION
    )
    return (states, attended)


def run_blocks(pieces, states):
    moved = tuple((jnp.moveaxis(piece_item, 1, 0) for piece_item in pieces))
    states, attended = lax.scan(block_step, states, moved)
    return (states, jnp.moveaxis(attended, 0, 1))


def gated_norm(attended, norm_gain, out_gate):
    root_mean = jnp.sqrt(jnp.mean(attended * attended, axis=-1, keepdims=True) + NORM_EPSILON)
    return attended / root_mean * norm_gain * jax.nn.silu(out_gate)


def compose(carried, block_piece):
    current_mapping, current_addend = carried
    segment_mapping, segment_addend = block_piece
    updated_mapping = jnp.einsum(
        "qfz,qze->qfe", segment_mapping, current_mapping, precision=TOP_PRECISION
    )
    updated_addend = (
        jnp.einsum("qfz,qze->qfe", segment_mapping, current_addend, precision=TOP_PRECISION)
        + segment_addend
    )
    return ((updated_mapping, updated_addend), None)


def delta_front(queries, key_vectors, values, write_strength, log_fading_factor, block_inverse):
    tracks, length, head_width = queries.shape
    pieces = block_parts(
        queries, key_vectors, values, write_strength, log_fading_factor, block_inverse
    )
    faded_queries, write_keys, write_values, faded_keys, causal, decays = pieces
    unit_matrix = jnp.eye(head_width, dtype=jnp.float32)
    identity_map = jnp.broadcast_to(unit_matrix, (tracks, head_width, head_width))
    block_maps = decays[..., None] * unit_matrix - jnp.einsum(
        "sbch,sbck->sbhk", faded_keys, write_keys, precision=TOP_PRECISION
    )
    block_adds = jnp.einsum("sbch,sbcv->sbhv", faded_keys, write_values, precision=TOP_PRECISION)
    (section_mapping, section_addend), _ = lax.scan(
        compose,
        (identity_map, jnp.zeros_like(identity_map)),
        (jnp.moveaxis(block_maps, 1, 0), jnp.moveaxis(block_adds, 1, 0)),
    )
    incoming_state = jnp.zeros_like(section_addend)
    for relay_turn in range(lax.axis_size("ctx") - 1):
        departing_state = (
            jnp.einsum("qfz,qze->qfe", section_mapping, incoming_state, precision=TOP_PRECISION)
            + section_addend
        )
        incoming_state = passed_along(departing_state.astype(jnp.bfloat16), "ctx", 1).astype(
            departing_state.dtype
        )
    return pieces, incoming_state


def named_and_rank(ranks, first, count, tokens):
    row = lax.broadcasted_iota(jnp.int32, (count, tokens), 0) + first
    named = jnp.zeros((count, tokens), jnp.bool_)
    for pick in range(ranks.shape[0]):
        named = jnp.logical_or(named, ranks[pick : pick + 1, :] == row)
    before = lax.broadcasted_iota(jnp.int32, (tokens, tokens), 0) < lax.broadcasted_iota(
        jnp.int32, (tokens, tokens), 1
    )
    earlier = jnp.dot(
        named.astype(jnp.float32).astype(jnp.bfloat16),
        before.astype(jnp.float32).astype(jnp.bfloat16),
        preferred_element_type=jnp.float32,
    )
    return named, earlier


def ranks_of(picks, owner_count, context_size):
    context = jnp.floor(picks.astype(jnp.float32) * (1.0 / owner_count)).astype(jnp.int32)
    return (picks - context * owner_count) * context_size + context


def pack_kernel(
    owner_count, context_size, blocks, picks_ref, hidden_ref, out_ref, spread_ref, result_ref, sent
):
    tokens, width = hidden_ref.shape
    parts = width // LANES
    per = CAPACITY * parts
    block = out_ref.shape[0] // blocks
    count = block // per
    ranks = ranks_of(picks_ref[...], owner_count, context_size)
    moves = []
    for i in range(blocks):
        named, earlier = named_and_rank(ranks, i * count, count, tokens)
        chosen = jnp.concatenate(
            [
                jnp.where(jnp.logical_and(named, earlier == slot), 1.0, 0.0)
                for slot in range(CAPACITY)
            ],
            axis=0,
        ).astype(jnp.bfloat16)
        rows = jnp.dot(chosen, hidden_ref[...], preferred_element_type=jnp.float32)
        for slot in range(CAPACITY):
            for part in range(parts):
                spread_ref[i, pl.ds(slot * parts + part, count, stride=per), :] = rows[
                    slot * count : (slot + 1) * count, part * LANES : (part + 1) * LANES
                ]
        result_ref[i] = spread_ref[i].astype(jnp.bfloat16)
        move = pltpu.make_async_copy(
            result_ref.at[i], out_ref.at[pl.ds(i * block, block), :], sent.at[i]
        )
        move.start()
        moves.append(move)
    for move in moves:
        move.wait()


def pack_rows(picks, hidden, owner_count, context_size, blocks):
    tokens, width = hidden.shape
    experts = owner_count * context_size
    rows = experts * CAPACITY * width // LANES
    here = pl.BlockSpec(memory_space=pltpu.VMEM)
    return pl.pallas_call(
        functools.partial(pack_kernel, owner_count, context_size, blocks),
        out_shape=pltpu.HBM((rows, LANES), jnp.bfloat16),
        in_specs=[here, here],
        out_specs=pl.BlockSpec(memory_space=pl.ANY),
        scratch_shapes=[
            pltpu.VMEM((blocks, rows // blocks, LANES), jnp.float32),
            pltpu.VMEM((blocks, rows // blocks, LANES), jnp.bfloat16),
            pltpu.SemaphoreType.DMA((blocks,)),
        ],
        compiler_params=pltpu.CompilerParams(vmem_limit_bytes=VMEM_BYTES),
        cost_estimate=pl.CostEstimate(
            flops=2 * experts * CAPACITY * tokens * width, bytes_accessed=rows * 256, transcendentals=0
        ),
        name="pack_rows",
    )(
        pltpu.with_memory_space_constraint(picks, pltpu.HBM),
        pltpu.with_memory_space_constraint(hidden, pltpu.HBM),
    )


def staging_kernel(*refs):
    count = len(refs) // 2
    ready = refs[-1]
    moves = [
        pltpu.make_async_copy(refs[i], refs[count + i], ready.at[i]) for i in range(count)
    ]
    for move in moves:
        move.start()
    for move in moves:
        move.wait()


def staged(arrays):
    there = pl.BlockSpec(memory_space=pl.ANY)
    here = pl.BlockSpec(memory_space=pltpu.VMEM)
    return pl.pallas_call(
        staging_kernel,
        out_shape=[pltpu.VMEM(array.shape, array.dtype) for array in arrays],
        in_specs=[there] * len(arrays),
        out_specs=[here] * len(arrays),
        scratch_shapes=[pltpu.SemaphoreType.DMA((len(arrays),))],
        cost_estimate=pl.CostEstimate(
            flops=0, bytes_accessed=4 * sum(array.size for array in arrays), transcendentals=0
        ),
        name="staged_weights",
    )(*[pltpu.with_memory_space_constraint(array, pltpu.HBM) for array in arrays])


def expert_kernel(
    blocks,
    received_there,
    gate_here,
    up_here,
    down_here,
    out_ref,
    received_ref,
    spread_ref,
    result_ref,
    ready,
    sent,
):
    width = gate_here.shape[0]
    parts = width // LANES
    per = CAPACITY * parts
    block = received_ref.shape[1]
    count = block // per
    loads = [
        pltpu.make_async_copy(
            received_there.at[pl.ds(i * block, block), :], received_ref.at[i], ready.at[i]
        )
        for i in range(blocks)
    ]
    for load in loads:
        load.start()
    def unpacked(i):
        loads[i].wait()
        spread_ref[i] = received_ref[i].astype(jnp.float32)
        return jnp.concatenate(
            [
                jnp.concatenate(
                    [
                        spread_ref[i, pl.ds(slot * parts + part, count, stride=per), :].astype(
                            jnp.bfloat16
                        )
                        for part in range(parts)
                    ],
                    axis=1,
                )
                for slot in range(CAPACITY)
            ],
            axis=0,
        )

    rows = unpacked(0)
    moves = []
    for i in range(blocks):
        gate = jnp.dot(rows, gate_here[...], preferred_element_type=jnp.float32)
        up = jnp.dot(rows, up_here[...], preferred_element_type=jnp.float32)
        if i + 1 < blocks:
            rows = unpacked(i + 1)
        active = (gate / (1.0 + jnp.exp(-gate)) * up).astype(jnp.bfloat16)
        produced = jnp.dot(active, down_here[...], preferred_element_type=jnp.float32)
        for slot in range(CAPACITY):
            for part in range(parts):
                spread_ref[i, pl.ds(slot * parts + part, count, stride=per), :] = produced[
                    slot * count : (slot + 1) * count, part * LANES : (part + 1) * LANES
                ]
        for half in range(2):
            at = pl.ds(half * (block // 2), block // 2)
            result_ref[i, at, :] = spread_ref[i, at, :].astype(jnp.bfloat16)
            move = pltpu.make_async_copy(
                result_ref.at[i, at, :],
                out_ref.at[pl.ds(i * block + half * (block // 2), block // 2), :],
                sent.at[2 * i + half],
            )
            move.start()
            moves.append(move)
    for move in moves:
        move.wait()


def expert_rows(received, gate_weights, up_weights, down_weights, blocks):
    rows = received.shape[0]
    width, units = gate_weights.shape
    slots = rows * LANES // width
    whole = pl.BlockSpec(memory_space=pl.ANY)
    here = pl.BlockSpec(memory_space=pltpu.VMEM)
    return pl.pallas_call(
        functools.partial(expert_kernel, blocks),
        out_shape=pltpu.HBM(received.shape, jnp.bfloat16),
        in_specs=[whole, here, here, here],
        out_specs=whole,
        scratch_shapes=[
            pltpu.VMEM((blocks, rows // blocks, LANES), jnp.bfloat16),
            pltpu.VMEM((blocks, rows // blocks, LANES), jnp.float32),
            pltpu.VMEM((blocks, rows // blocks, LANES), jnp.bfloat16),
            pltpu.SemaphoreType.DMA((blocks,)),
            pltpu.SemaphoreType.DMA((2 * blocks,)),
        ],
        compiler_params=pltpu.CompilerParams(vmem_limit_bytes=VMEM_BYTES),
        cost_estimate=pl.CostEstimate(
            flops=6 * slots * width * units,
            bytes_accessed=4 * rows * LANES + 6 * width * units,
            transcendentals=slots * units,
        ),
        name="expert_rows",
    )(received, gate_weights, up_weights, down_weights)


def combine_kernel(owner_count, context_size, picks_ref, weights_ref, returned_ref, out_ref, spread_ref, total_ref):
    tokens, width = out_ref.shape
    parts = width // LANES
    per = CAPACITY * parts
    count = returned_ref.shape[0] // per
    step = pl.program_id(0)

    @pl.when(step == 0)
    def _():
        total_ref[...] = jnp.zeros_like(total_ref)

    spread_ref[...] = returned_ref[...].astype(jnp.float32)
    ranks = ranks_of(picks_ref[...], owner_count, context_size)
    named, earlier = named_and_rank(ranks, step * count, count, tokens)
    row = lax.broadcasted_iota(jnp.int32, (count, tokens), 0) + step * count
    scale = jnp.zeros((count, tokens), jnp.float32)
    for pick in range(ranks.shape[0]):
        scale = jnp.where(ranks[pick : pick + 1, :] == row, weights_ref[pick : pick + 1, :], scale)
    high = scale.astype(jnp.bfloat16).astype(jnp.float32)
    halves = jnp.concatenate([high, scale - high], axis=1)
    at = jnp.concatenate([jnp.where(named, earlier, -1.0)] * 2, axis=1)
    table = jnp.concatenate(
        [jnp.where(at == slot, halves, 0.0) for slot in range(CAPACITY)], axis=0
    ).astype(jnp.bfloat16)
    rows = jnp.concatenate(
        [
            jnp.concatenate(
                [
                    spread_ref[pl.ds(slot * parts + part, count, stride=per), :].astype(jnp.bfloat16)
                    for part in range(parts)
                ],
                axis=1,
            )
            for slot in range(CAPACITY)
        ],
        axis=0,
    )
    both = lax.dot_general(
        table, rows, (((0,), (0,)), ((), ())), preferred_element_type=jnp.float32
    )
    total = total_ref[...] + (both[:tokens] + both[tokens:])
    total_ref[...] = total

    @pl.when(step == pl.num_programs(0) - 1)
    def _():
        out_ref[...] = total.astype(jnp.bfloat16)


def combine_rows(picks, weights, returned, owner_count, context_size, width, steps):
    tokens = picks.shape[1]
    rows = returned.shape[0]
    return pl.pallas_call(
        functools.partial(combine_kernel, owner_count, context_size),
        grid=(steps,),
        out_shape=jax.ShapeDtypeStruct((tokens, width), jnp.bfloat16),
        in_specs=[
            pl.BlockSpec(picks.shape, lambda i: (0, 0)),
            pl.BlockSpec(weights.shape, lambda i: (0, 0)),
            pl.BlockSpec((rows // steps, LANES), lambda i: (i, 0)),
        ],
        out_specs=pl.BlockSpec((tokens, width), lambda i: (0, 0)),
        scratch_shapes=[
            pltpu.VMEM((rows // steps, LANES), jnp.float32),
            pltpu.VMEM((tokens, width), jnp.float32),
        ],
        compiler_params=pltpu.CompilerParams(vmem_limit_bytes=VMEM_BYTES),
        cost_estimate=pl.CostEstimate(
            flops=4 * rows * LANES * tokens, bytes_accessed=2 * rows * LANES, transcendentals=0
        ),
        name="combine_rows",
    )(picks, weights, returned)


def exchange(rows):
    return lax.all_to_all(rows, ("exp", "ctx"), split_axis=0, concat_axis=0, tiled=True)


def body(
    queries,
    key_vectors,
    values,
    out_gate,
    write_strength,
    log_fading_factor,
    block_inverse,
    norm_gain,
    hidden,
    routes,
    route_weights,
    gate_weights,
    up_weights,
    down_weights,
):
    width = hidden.shape[1]
    context_size = lax.axis_size("ctx")
    owner_count = lax.axis_size("exp")
    picks = routes.T
    outgoing = pack_rows(picks, hidden, owner_count, context_size, 4)
    received = exchange(outgoing)
    pieces, incoming_state = delta_front(
        queries, key_vectors, values, write_strength, log_fading_factor, block_inverse
    )
    weights = staged([gate_weights[0], up_weights[0], down_weights[0]])
    received, incoming_state, weights = lax.optimization_barrier(
        (received, incoming_state, weights)
    )
    produced = expert_rows(received, *weights, 4)
    returned = exchange(produced)
    expert_output = combine_rows(
        picks, route_weights.T, returned, owner_count, context_size, width, 1
    )
    _, attended = run_blocks(pieces, incoming_state)
    mixer_output = gated_norm(attended.reshape(out_gate.shape), norm_gain, out_gate)
    return (mixer_output, expert_output)


def solution(mesh):
    placed = (
        P("exp", "ctx", None),
        P("exp", "ctx", None),
        P("exp", "ctx", None),
        P("exp", "ctx", None),
        P("exp", "ctx"),
        P("exp", "ctx"),
        P("exp", "ctx", None, None),
        P(),
        P(("ctx", "exp"), None),
        P(("ctx", "exp"), None),
        P(("ctx", "exp"), None),
        P(("ctx", "exp"), None, None),
        P(("ctx", "exp"), None, None),
        P(("ctx", "exp"), None, None),
    )
    return jax.shard_map(
        body,
        mesh=mesh,
        in_specs=placed,
        out_specs=(P("exp", "ctx", None), P(("ctx", "exp"), None)),
        check_vma=False,
    )
```
